32 devices in a mesh: dp: 8 (over y, x, core), mp: 4 (over z).
Axes of the slice: x: 2, y: 2, z: 4, core: 2. Of those that a mesh axis runs over, the one named last changes fastest.
Arguments:
- activations: bfloat16 [8192, 1024], P(('dp', 'mp')), may hold values from -6 to 6
- lengths: int32 [8, 4], P('dp'), may hold values from 1 to 1024, as said below
- cotangent: bfloat16 [8192, 1024], P(('dp', 'mp')), may hold values from -6 to 6
- gain_attn: float32 [2, 1024], replicated, may hold values from 0.5 to 1.5
- shift_attn: float32 [2, 1024], replicated, may hold values from -3 to 3
- w_query: bfloat16 [2, 1024, 1024], P(None, None, 'mp'), may hold values from -0.1875 to 0.1875
- b_query: float32 [2, 1024], P(None, 'mp'), may hold values from -3 to 3
- w_key: bfloat16 [2, 1024, 1024], P(None, None, 'mp'), may hold values from -0.1875 to 0.1875
- w_value: bfloat16 [2, 1024, 1024], P(None, None, 'mp'), may hold values from -0.1875 to 0.1875
- b_value: float32 [2, 1024], P(None, 'mp'), may hold values from -3 to 3
- w_out: bfloat16 [2, 1024, 1024], P(None, 'mp'), may hold values from -0.75 to 0.75
- b_out: float32 [2, 1024], replicated, may hold values from -3 to 3
- gain_ffn: float32 [2, 1024], replicated, may hold values from 0.5 to 1.5
- shift_ffn: float32 [2, 1024], replicated, may hold values from -3 to 3
- w_up: bfloat16 [2, 1024, 4096], P(None, None, 'mp'), may hold values from -0.1875 to 0.1875
- b_up: float32 [2, 4096], replicated, may hold values from -3 to 3
- w_down: bfloat16 [2, 4096, 1024], P(None, 'mp'), may hold values from -0.09375 to 0.09375
- b_down: float32 [2, 1024], replicated, may hold values from -3 to 3
Outputs:
- activations_out: bfloat16 [8192, 1024], P(('dp', 'mp'))
- input_grad: bfloat16 [8192, 1024], P(('dp', 'mp'))
- grad_gain_attn: float32 [2, 1024], replicated
- grad_shift_attn: float32 [2, 1024], replicated
- grad_w_query: float32 [2, 1024, 1024], P(None, None, 'mp')
- grad_b_query: float32 [2, 1024], P(None, 'mp')
- grad_w_key: float32 [2, 1024, 1024], P(None, None, 'mp')
- grad_w_value: float32 [2, 1024, 1024], P(None, None, 'mp')
- grad_b_value: float32 [2, 1024], P(None, 'mp')
- grad_w_out: float32 [2, 1024, 1024], P(None, 'mp')
- grad_b_out: float32 [2, 1024], replicated
- grad_gain_ffn: float32 [2, 1024], replicated
- grad_shift_ffn: float32 [2, 1024], replicated
- grad_w_up: float32 [2, 1024, 4096], P(None, None, 'mp')
- grad_b_up: float32 [2, 4096], P(None, 'mp')
- grad_w_down: float32 [2, 4096, 1024], P(None, 'mp')
- grad_b_down: float32 [2, 1024], replicated
The draws below stay inside these ranges and needn't reach their ends.
Inputs may be any that keep to these rules, and one draw needn't show every extreme that they name: Each row holds 4 lengths that sum to 1024; one of them, at a place drawn from the seed, is more than 768, the others are under 256 / 4.
All inputs are finite; a program needn't handle non-finite values.
Results may differ from the reference program's by a relative error of at most 0.024.
Values may be sent and summed in bfloat16 or wider, within the bound.
No kernel may reach another device: no remote copies, remote signals or barrier semaphores. Data moves between devices by JAX's collectives and lax.ppermute only.
A program may use at most 192 MiB of HBM per device.

```python
import jax
import jax.numpy as jnp
from jax import lax

D = 1024
H = 8
HD = 128
FF = 4096
LAYERS = 2
SEGS = 4
TOK_DEV = 256
GROUP = 1024
GROUPS = 8
TOKENS = 8192


def draw_lengths(key, part):
    key = jax.random.fold_in(key, 7)
    short_key, place_key = jax.random.split(key)
    shorts = jax.random.randint(short_key, (GROUPS, SEGS - 1), 1, TOK_DEV // SEGS, dtype=jnp.int32)
    longest = GROUP - jnp.sum(shorts, axis=1)
    long_slot = jax.random.randint(place_key, (GROUPS,), 0, SEGS, dtype=jnp.int32)
    columns = jnp.arange(SEGS, dtype=jnp.int32)
    source = columns[None, :] - (columns[None, :] > long_slot[:, None]).astype(jnp.int32)
    source = jnp.clip(source, 0, SEGS - 2)
    picked = jnp.take_along_axis(shorts, source, axis=1)
    return jnp.where(columns[None, :] == long_slot[:, None], longest[:, None], picked)


def block_scale(rng, shape, cuts, smallest, largest):
    def one(position, parts):
        steps = jax.random.uniform(jax.random.fold_in(jax.random.fold_in(rng, 6), position), (parts,), jnp.float32, smallest / len(cuts), largest / len(cuts))
        return jnp.repeat(jnp.exp(steps), shape[position] // parts).reshape((-1,) + (1,) * (len(shape) - position - 1))

    loudness = one(*cuts[0])
    for cut in cuts[1:]:
        loudness = loudness * one(*cut)
    return loudness


def normal_values(rng, dims, scale, bound, shards=(), kind=jnp.bfloat16):
    array = jax.random.normal(rng, dims, jnp.float32) * scale
    if len(shards) > 0:
        array = block_scale(rng, dims, shards, -0.22, 0.18) * array
    return jnp.clip(array, min=-bound, max=bound).astype(kind)


def setup_inputs(seed: int = 0) -> dict:
    streams_of = jax.random.split(jax.random.key(seed), 19)
    activations = normal_values(streams_of[0], (TOKENS, D), 1.0, 6.0, ((0, 32),))
    lengths = draw_lengths(jax.random.fold_in(streams_of[18], 71), 0)
    cotangent = normal_values(streams_of[2], (TOKENS, D), 1.0, 6.0, ((0, 32),))
    gain_attn = jnp.clip(1.0 + 0.1 * jax.random.normal(streams_of[3], (LAYERS, D), jnp.float32), 0.5, 1.5)
    shift_attn = normal_values(streams_of[4], (LAYERS, D), 0.5, 3.0, (), jnp.float32)
    w_query = normal_values(streams_of[5], (LAYERS, D, D), D ** -0.5, 0.1875, ((2, 4),))
    b_query = normal_values(streams_of[6], (LAYERS, D), 0.5, 3.0, ((1, 4),), jnp.float32)
    w_key = normal_values(streams_of[7], (LAYERS, D, D), D ** -0.5, 0.1875, ((2, 4),))
    w_value = normal_values(streams_of[8], (LAYERS, D, D), D ** -0.5, 0.1875, ((2, 4),))
    b_value = normal_values(streams_of[9], (LAYERS, D), 0.5, 3.0, ((1, 4),), jnp.float32)
    w_out = normal_values(streams_of[10], (LAYERS, D, D), (D // 16) ** -0.5, 0.75, ((1, 4),))
    b_out = normal_values(streams_of[11], (LAYERS, D), 0.5, 3.0, (), jnp.float32)
    gain_ffn = jnp.clip(1.0 + 0.1 * jax.random.normal(streams_of[12], (LAYERS, D), jnp.float32), 0.5, 1.5)
    shift_ffn = normal_values(streams_of[13], (LAYERS, D), 0.5, 3.0, (), jnp.float32)
    w_up = normal_values(streams_of[14], (LAYERS, D, FF), D ** -0.5, 0.1875, ((2, 4),))
    b_up = normal_values(streams_of[15], (LAYERS, FF), 0.5, 3.0, (), jnp.float32)
    w_down = normal_values(streams_of[16], (LAYERS, FF, D), FF ** -0.5, 0.09375, ((1, 4),))
    b_down = normal_values(streams_of[17], (LAYERS, D), 0.5, 3.0, (), jnp.float32)
    return dict(activations=activations, lengths=lengths, cotangent=cotangent, gain_attn=gain_attn, shift_attn=shift_attn, w_query=w_query, b_query=b_query, w_key=w_key, w_value=w_value, b_value=b_value, w_out=w_out, b_out=b_out, gain_ffn=gain_ffn, shift_ffn=shift_ffn, w_up=w_up, b_up=b_up, w_down=w_down, b_down=b_down)


precise = lax.Precision.HIGHEST
norm_eps = 1e-05

@jax.custom_vjp
def low(v):
    return lax.optimization_barrier(v.astype(jnp.bfloat16)).astype(jnp.float32)

@jax.custom_vjp
def low_back(v):
    return v

def low_keep(v):
    return (low(v), None)

def low_pass(kept, grad):
    return (grad,)

def back_keep(v):
    return (v, None)

def back_low(kept, grad):
    return (low(grad),)
low.defvjp(low_keep, low_pass)
low_back.defvjp(back_keep, back_low)

def rounded_both(values):
    return low(low_back(values))

def product(left, right):
    return jnp.dot(left, right, precision=precise)

def layer_norm(stream, gain, shift):
    centred = stream - lax.optimization_barrier(jnp.mean(stream, axis=-1, keepdims=True))
    spread = lax.optimization_barrier(jnp.mean(centred * centred, axis=-1, keepdims=True))
    return centred * lax.rsqrt(spread + norm_eps) * gain + shift

def segment_ids(row_lengths, total_rows):
    doc_ends = jnp.cumsum(row_lengths)
    positions = jnp.arange(total_rows, dtype=jnp.int32)
    return lax.optimization_barrier(jnp.sum((positions[:, None] >= doc_ends[None, :]).astype(jnp.int32), axis=1))

def group_attention(query_rows, key_rows, value_rows, segments, slopes):
    block_rows = min(512, GROUP)
    block_count = GROUP // block_rows
    score_scale = HD ** (-0.5)
    positions = jnp.arange(GROUP, dtype=jnp.int32)

    def one_block(block_index):
        begin_row = block_index * block_rows
        query_block = lax.dynamic_slice_in_dim(query_rows, begin_row, block_rows, 0)
        query_pos = lax.dynamic_slice_in_dim(positions, begin_row, block_rows, 0)
        query_seg = lax.dynamic_slice_in_dim(segments, begin_row, block_rows, 0)
        logits = jnp.einsum('qhd,khd->hqk', query_block, key_rows, precision=precise) * score_scale
        distance = (query_pos[:, None] - positions[None, :]).astype(jnp.float32)
        logits = logits - slopes[:, None, None] * distance[None]
        allowed = (query_seg[:, None] == segments[None, :]) & (positions[None, :] <= query_pos[:, None])
        scores = low_back(jnp.where(allowed[None], logits, -1e+30))
        row_max = lax.optimization_barrier(jnp.max(scores, axis=-1, keepdims=True))
        weights = jnp.exp(scores - row_max)
        probabilities = weights / lax.optimization_barrier(jnp.sum(weights, axis=-1, keepdims=True))
        return jnp.einsum('hqk,khd->qhd', low(probabilities), value_rows, precision=precise)
    blocks = lax.map(jax.checkpoint(one_block), jnp.arange(block_count, dtype=jnp.int32))
    return blocks.reshape(GROUP, H, HD)

def forward(stream, params, seg_all, slopes):
    for layer_index in range(LAYERS):
        gain_attn, shift_attn, w_query, b_query, w_key, w_value, b_value, w_out, b_out, gain_ffn, shift_ffn, w_up, b_up, w_down, b_down = [member[layer_index] for member in params]
        normed = low(layer_norm(stream, gain_attn, shift_attn))
        queries = rounded_both(product(normed, w_query) + b_query)
        key_proj = rounded_both(product(normed, w_key))
        value_proj = rounded_both(product(normed, w_value) + b_value)

        def per_group(pieces):
            return group_attention(pieces[0], pieces[1], pieces[2], pieces[3], slopes)
        mixed = lax.map(per_group, (queries.reshape(GROUPS, GROUP, H, HD), key_proj.reshape(GROUPS, GROUP, H, HD), value_proj.reshape(GROUPS, GROUP, H, HD), seg_all))
        mixed = rounded_both(mixed.reshape(TOKENS, D))
        middle = stream + low_back(product(mixed, w_out) + b_out)
        normed_mid = low(layer_norm(middle, gain_ffn, shift_ffn))
        hidden = low_back(product(normed_mid, w_up) + b_up)
        active = low(jax.nn.gelu(hidden, approximate=True))
        stream = middle + low_back(product(active, w_down) + b_down)
    return stream

def reference(activations, lengths, cotangent, gain_attn, shift_attn, w_query, b_query, w_key, w_value, b_value, w_out, b_out, gain_ffn, shift_ffn, w_up, b_up, w_down, b_down):
    head_ids = jnp.arange(H, dtype=jnp.float32)
    slopes = 2.0 ** (-8.0 * (head_ids + 1.0) / H)
    seg_all = jax.vmap(lambda row_lengths: segment_ids(row_lengths, GROUP))(lengths)
    params = tuple((member.astype(jnp.float32) for member in (gain_attn, shift_attn, w_query, b_query, w_key, w_value, b_value, w_out, b_out, gain_ffn, shift_ffn, w_up, b_up, w_down, b_down)))

    def run(stream, weights):
        return forward(stream, weights, seg_all, slopes)
    result, pullback = jax.vjp(run, activations.astype(jnp.float32), params)
    grad_input, grads = pullback(cotangent.astype(jnp.float32))
    return (result.astype(jnp.bfloat16), grad_input.astype(jnp.bfloat16), grads[0], grads[1], grads[2], grads[3], grads[4], grads[5], grads[6], grads[7], grads[8], grads[9], grads[10], grads[11], grads[12], grads[13], grads[14])
```

```python
import functools

import jax
import jax.numpy as jnp
from jax import lax
from jax.experimental import pallas as pl
from jax.experimental.pallas import tpu as pltpu
from jax.sharding import Mesh
from jax.sharding import PartitionSpec as P

H = 8
HD = 128
LAYERS = 2
norm_eps = 1e-05
F32 = jnp.float32
BF16 = jnp.bfloat16


def gelu_tanh(values):
    return jax.nn.gelu(values, approximate=True)


def norm_parts(stream):
    centred = stream - jnp.mean(stream, axis=-1, keepdims=True)
    inverse = lax.rsqrt(jnp.mean(centred * centred, axis=-1, keepdims=True) + norm_eps)
    return centred * inverse, inverse


def norm_back(grad_normed, unit_rows, inverse, gain):
    scaled = grad_normed * gain
    return inverse * (
        scaled
        - jnp.mean(scaled, axis=-1, keepdims=True)
        - unit_rows * jnp.mean(scaled * unit_rows, axis=-1, keepdims=True)
    )


def dot(left, right):
    return jnp.dot(left, right, preferred_element_type=F32)


def dot_nt(left, right):
    return jnp.einsum("ti,oi->to", left, right, preferred_element_type=F32)


def dot_tn(left, right):
    return jnp.einsum("ti,to->io", left, right, preferred_element_type=F32)


def after(value, *others):
    return lax.optimization_barrier((value,) + others)[0]


def swap(value, axis):
    return lax.ppermute(value, axis, [(0, 1), (1, 0)])


def swap_one(value, axes):
    return lax.ppermute(value, axes, [(2, 3), (3, 2)])


def gather_rows(rows):
    if lax.axis_size("r") == 2:
        across = swap(rows, "r")
        beside = swap(rows, "c")
        return jnp.concatenate([rows, across, beside, swap(across, "c")], 0)
    mine = lax.all_gather(rows, "r", axis=0, tiled=True)
    return jnp.concatenate([mine, swap(mine, "c")], 0)


def axis_order(axis):
    size = lax.axis_size(axis)
    if size == 2:
        return [lax.axis_index(axis), 1 - lax.axis_index(axis)]
    return list(range(size))


def row_places(chunk, rows):
    pieces = []
    across = lax.axis_size("r")
    for core in axis_order("c"):
        for place in axis_order("r"):
            pieces.append(((chunk * across + place) * 2 + core) * rows + jnp.arange(rows, dtype=jnp.int32))
    return jnp.concatenate(pieces)


def scatter_rows(partial):
    half = partial.shape[0] // 2
    beside = swap(partial[half:], "c")
    if lax.axis_size("r") == 2:
        rows = half // 2
        send = (partial[rows:half].astype(F32) + beside[rows:].astype(F32)).astype(BF16)
        across = swap(send, "r")
        return partial[:rows].astype(F32) + beside[:rows].astype(F32) + across.astype(F32)
    total = (partial[:half].astype(F32) + beside.astype(F32)).astype(BF16)
    return lax.psum_scatter(total, "r", scatter_dimension=0, tiled=True).astype(F32)


def to_chunks(value):
    half = value.shape[0] // 2
    low, high = value[:half], value[half:]
    core, block = lax.axis_index("c"), lax.axis_index("b")
    first = jnp.where(block == 0, low, high)
    second = jnp.where(block == 0, high, low)
    first = lax.ppermute(first, ("c", "b"), [(0, 0), (1, 2), (2, 1), (3, 3)])
    second = lax.ppermute(second, ("c", "b"), [(0, 2), (1, 0), (2, 3), (3, 1)])
    return [jnp.where(core == 0, first, second), jnp.where(core == 0, second, first)]


def from_chunks(chunks):
    core, block = lax.axis_index("c"), lax.axis_index("b")
    first = jnp.where(core == 0, chunks[0], chunks[1])
    second = jnp.where(core == 0, chunks[1], chunks[0])
    first = lax.ppermute(first, ("c", "b"), [(0, 0), (2, 1), (1, 2), (3, 3)])
    second = lax.ppermute(second, ("c", "b"), [(2, 0), (0, 1), (3, 2), (1, 3)])
    low = jnp.where(block == 0, first, second)
    high = jnp.where(block == 0, second, first)
    return jnp.concatenate([low, high], 0)


def gather_axis(pieces, axis, only_last):
    size = lax.axis_size(axis)
    if size == 2:
        if only_last:
            other = [lax.ppermute(piece, (axis, "c"), [(1, 3), (3, 1)]) for piece in pieces]
        else:
            other = [swap(piece, axis) for piece in pieces]
        return [pieces, other]
    whole = [lax.all_gather(piece, axis, axis=0) for piece in pieces]
    return [[piece[place] for piece in whole] for place in range(size)]


def gather_plane(piece, axes, only_last):
    inner = [group[0] for group in gather_axis([piece], axes[1], only_last)]
    outer = gather_axis(inner, axes[0], only_last)
    width = lax.axis_size(axes[1])
    pieces, places = [], []
    for slow, group in zip(axis_order(axes[0]), outer):
        for fast, member in zip(axis_order(axes[1]), group):
            pieces.append(member)
            places.append(slow * width + fast)
    return pieces, places


def plane_place(axes):
    return lax.axis_index(axes[0]) * lax.axis_size(axes[1]) + lax.axis_index(axes[1])


def reduce_half(value, axis):
    if lax.axis_size(axis) == 2:
        index = lax.axis_index(axis)
        send = lax.dynamic_index_in_dim(value, 1 - index, 0, keepdims=False)
        keep = lax.dynamic_index_in_dim(value, index, 0, keepdims=False)
        return keep.astype(F32) + swap(send, axis).astype(F32)
    return lax.psum_scatter(value, axis, scatter_dimension=0, tiled=False).astype(F32)


def sum_small(value):
    for axis in ("c", "kx", "ky", "r", "b"):
        if lax.axis_size(axis) == 2:
            value = value + swap(value, axis)
        else:
            value = lax.psum(value, axis)
    return value


def place_kernel(count, rows, info, *refs):
    own, pieces, out, sems = refs[0], refs[1 : 1 + count], refs[1 + count], refs[2 + count]

    @pl.when(info[0] == 0)
    def _():
        copy = pltpu.make_async_copy(own, out, sems.at[0])
        copy.start()
        copy.wait()

    @pl.when(info[0] != 0)
    def _():
        copies = []
        for index in range(count):
            begin = pl.multiple_of(info[1 + index] * rows, rows)
            copies.append(pltpu.make_async_copy(pieces[index], out.at[pl.ds(begin, rows)], sems.at[index]))
        for copy in copies:
            copy.start()
        for copy in copies:
            copy.wait()


def place_pieces(own, pieces, places):
    count, rows = len(pieces), pieces[0].shape[0]
    core = lax.axis_index("c")
    info = jnp.stack([jnp.asarray(v, jnp.int32) for v in [core] + places])
    return pl.pallas_call(
        functools.partial(place_kernel, count, rows),
        out_shape=jax.ShapeDtypeStruct(own.shape, own.dtype),
        in_specs=[pl.BlockSpec(memory_space=pltpu.SMEM)] + [pl.BlockSpec(memory_space=pl.ANY)] * (1 + count),
        out_specs=pl.BlockSpec(memory_space=pl.ANY),
        scratch_shapes=[pltpu.SemaphoreType.DMA((count,))],
        cost_estimate=pl.CostEstimate(flops=0, bytes_accessed=2 * own.size * 2, transcendentals=0),
    )(info, own, *pieces)


def start_fetch(own, axes):
    count = lax.axis_size("ky") * lax.axis_size("kx")
    rows = own.shape[0] // count
    return lax.dynamic_slice_in_dim(own, plane_place(axes) * rows, rows, 0)


def finish_fetch(own, piece, axes):
    pieces, places = gather_plane(piece, axes, True)
    return place_pieces(own, pieces, places)


def reduce_plane(grad, axes):
    outer, inner = lax.axis_size(axes[0]), lax.axis_size(axes[1])
    rows, cols = grad.shape
    part = rows // (outer * inner)
    value = reduce_half(grad.reshape(outer, inner * part, cols), axes[0]).astype(BF16)
    value = reduce_half(value.reshape(inner, part, cols), axes[1])
    return value


def reduce_pair(value):
    core = lax.axis_index("c")
    half = value.shape[0] // 2
    low, high = value[:half], value[half:]
    send = jnp.where(core == 0, high, low).astype(BF16)
    got = lax.ppermute(send, ("c", "b"), [(2, 1), (3, 0), (0, 2), (1, 3)])
    far = swap_one(high.astype(BF16), ("c", "b"))
    return (jnp.where(core == 0, low, far.astype(F32)) + got.astype(F32)).astype(BF16)


def spread_weight(piece, axes):
    pieces, places = gather_plane(piece, axes, False)
    core = lax.axis_index("c")
    beside = [swap(member, "c") for member in pieces]
    return (
        pieces + beside,
        [place * 2 + core for place in places] + [place * 2 + 1 - core for place in places],
    )


def store_kernel(count, rows, column, layer, info, *refs):
    pieces = refs[:count]
    out, loaded, ready, in_sems, out_sems = refs[-5], refs[-4], refs[-3], refs[-2], refs[-1]
    width = out.shape[2]
    loads, stores = [], []
    for index in range(count):
        source = pieces[index].at[:, pl.ds(column, width)]
        loads.append(pltpu.make_async_copy(source, loaded.at[index], in_sems.at[index]))
        begin = pl.multiple_of(info[index] * rows, rows)
        stores.append(
            pltpu.make_async_copy(ready.at[index], out.at[layer, pl.ds(begin, rows)], out_sems.at[index])
        )
    for load in loads:
        load.start()
    for index in range(count):
        loads[index].wait()
        ready[index] = loaded[index].astype(F32)
        stores[index].start()
    for store in stores:
        store.wait()


def store_pieces(pieces, places, column, width, layer, before):
    count, rows = len(pieces), pieces[0].shape[0]
    info = jnp.stack([jnp.asarray(v, jnp.int32) for v in places])
    shape = jax.ShapeDtypeStruct((LAYERS, count * rows, width), F32)
    given = [] if before is None else [before]
    size = count * rows * width
    return pl.pallas_call(
        functools.partial(store_kernel, count, rows, column, layer),
        out_shape=shape,
        in_specs=[pl.BlockSpec(memory_space=pltpu.SMEM)]
        + [pl.BlockSpec(memory_space=pl.ANY)] * (count + len(given)),
        out_specs=pl.BlockSpec(memory_space=pl.ANY),
        scratch_shapes=[
            pltpu.VMEM((count, rows, width), BF16),
            pltpu.VMEM((count, rows, width), F32),
            pltpu.SemaphoreType.DMA((count,)),
            pltpu.SemaphoreType.DMA((count,)),
        ],
        input_output_aliases={} if before is None else {1 + count: 0},
        compiler_params=pltpu.CompilerParams(vmem_limit_bytes=size * 6 + (4 << 20)),
        cost_estimate=pl.CostEstimate(flops=0, bytes_accessed=size * 6, transcendentals=0),
    )(info, *pieces, *given)


def chunk_scores(query_heads, key_heads, query_pos, key_pos, query_seg, key_seg, slopes):
    logits = jnp.einsum("qhd,khd->hqk", query_heads, key_heads, preferred_element_type=F32) * HD ** (-0.5)
    distance = (query_pos[:, None] - key_pos[None, :]).astype(F32)
    logits = logits - slopes[:, None, None] * distance[None]
    allowed = (query_seg[:, None] == key_seg[None, :]) & (key_pos[None, :] <= query_pos[:, None])
    return jnp.where(allowed[None], logits, -1e30)


def heads_of(rows):
    return rows.reshape(rows.shape[0], -1, HD)


def attend(query, key, value, places, slopes):
    scores = chunk_scores(heads_of(query), heads_of(key), *places, slopes)
    row_max = jnp.max(scores, axis=-1, keepdims=True)
    weights = jnp.exp(scores - row_max)
    totals = jnp.sum(weights, axis=-1, keepdims=True)
    probabilities = (weights / totals).astype(BF16)
    mixed = jnp.einsum("hqk,khd->qhd", probabilities, heads_of(value), preferred_element_type=F32)
    return mixed.reshape(query.shape).astype(BF16), row_max + jnp.log(totals)


def attend_back(query, key, value, places, slopes, log_totals, grad_mixed):
    scale = HD ** (-0.5)
    query_heads, key_heads, value_heads, grad_heads = map(heads_of, (query, key, value, grad_mixed))
    scores = chunk_scores(query_heads, key_heads, *places, slopes)
    probabilities = jnp.exp(scores - log_totals)
    rounded = probabilities.astype(BF16)
    grad_value = jnp.einsum("hqk,qhd->khd", rounded, grad_heads, preferred_element_type=F32)
    grad_probs = jnp.einsum("qhd,khd->hqk", grad_heads, value_heads, preferred_element_type=F32)
    centre = jnp.sum(grad_probs * probabilities, axis=-1, keepdims=True)
    grad_scores = (probabilities * (grad_probs - centre)).astype(BF16)
    grad_query = jnp.einsum("hqk,khd->qhd", grad_scores, key_heads, preferred_element_type=F32) * scale
    grad_key = jnp.einsum("hqk,qhd->khd", grad_scores, query_heads, preferred_element_type=F32) * scale
    return (
        grad_query.reshape(query.shape).astype(BF16),
        grad_key.reshape(key.shape),
        grad_value.reshape(value.shape),
    )


def local(
    activations,
    lengths,
    cotangent,
    gain_attn,
    shift_attn,
    w_query,
    b_query,
    w_key,
    w_value,
    b_value,
    w_out,
    b_out,
    gain_ffn,
    shift_ffn,
    w_up,
    b_up,
    w_down,
    b_down,
):
    core, block, place = lax.axis_index("c"), lax.axis_index("b"), lax.axis_index("r")
    across = lax.axis_size("r")
    shard = ((block + core) % 2) * across + place
    home = block * across + place
    rows = activations.shape[0] // 2
    head_width = w_query.shape[2]
    head_count = head_width // HD
    hidden_width = w_up.shape[2]

    doc_ends = jnp.cumsum(jnp.where(core == block, lengths[0], swap(lengths[0], "c")))
    places, segments = [], []
    for chunk in range(2):
        spots = row_places(chunk, rows)
        places.append(spots)
        segments.append(jnp.sum((spots[:, None] >= doc_ends[None, :]).astype(jnp.int32), axis=1))
    places_both = jnp.concatenate(places)
    segments_both = jnp.concatenate(segments)
    spot_sets = [
        (places[0], places[0], segments[0], segments[0]),
        (places[1], places_both, segments[1], segments_both),
    ]
    head_ids = (shard * head_count + jnp.arange(head_count, dtype=jnp.int32)).astype(F32)
    slopes = 2.0 ** (-8.0 * (head_ids + 1.0) / H)

    streams = [value.astype(F32) for value in to_chunks(activations)]

    bias_own = jnp.concatenate([b_query, b_value], 1)
    bias_use = jnp.where(core == 0, bias_own, swap_one(bias_own, ("c", "b")))
    zero = jnp.zeros((head_width,), F32)
    bias_qkv = [
        jnp.concatenate([bias_use[layer, :head_width], zero, bias_use[layer, head_width:]])
        for layer in range(LAYERS)
    ]
    bias_up = [
        lax.dynamic_slice_in_dim(b_up[layer], shard * hidden_width, hidden_width, 0) for layer in range(LAYERS)
    ]

    yx, xy = ("ky", "kx"), ("kx", "ky")
    used = []
    previous = streams[0]
    for layer in range(LAYERS):
        owns = [
            (jnp.concatenate([w_query[layer], w_key[layer], w_value[layer]], 1), yx),
            (w_out[layer], xy),
            (w_up[layer], yx),
            (w_down[layer], xy),
        ]
        members = []
        for own, axes in owns:
            piece = after(start_fetch(own, axes), previous)
            piece = swap_one(piece, ("c", "b"))
            previous = piece
            members.append(finish_fetch(own, piece, axes))
        used.append(members)

    stored = []
    for layer in range(LAYERS):
        weight_qkv, weight_out, weight_up, weight_down = used[layer]
        saved = []
        for chunk in range(2):
            stream = streams[chunk]
            unit, inverse = norm_parts(stream)
            normed = (unit * gain_attn[layer] + shift_attn[layer]).astype(BF16)
            inputs = gather_rows(normed)
            qkv = (dot(inputs, weight_qkv) + bias_qkv[layer]).astype(BF16)
            query, key, value = (
                qkv[:, :head_width],
                qkv[:, head_width : 2 * head_width],
                qkv[:, 2 * head_width :],
            )
            if chunk == 1:
                key = jnp.concatenate([saved[0][4], key], 0)
                value = jnp.concatenate([saved[0][5], value], 0)
            mixed, log_totals = attend(query, key, value, spot_sets[chunk], slopes)
            middle = stream + (scatter_rows(dot(mixed, weight_out).astype(BF16)) + b_out[layer])
            unit_mid, inverse_mid = norm_parts(middle)
            normed_mid = (unit_mid * gain_ffn[layer] + shift_ffn[layer]).astype(BF16)
            inputs_mid = gather_rows(normed_mid)
            hidden = dot(inputs_mid, weight_up) + bias_up[layer]
            active = gelu_tanh(hidden).astype(BF16)
            streams[chunk] = middle + (scatter_rows(dot(active, weight_down).astype(BF16)) + b_down[layer])
            saved.append(
                (
                    unit,
                    inverse,
                    inputs,
                    query,
                    key,
                    value,
                    mixed,
                    log_totals,
                    unit_mid,
                    inverse_mid,
                    inputs_mid,
                    hidden,
                    active,
                )
            )
        stored.append(saved)
    activations_out = from_chunks([value.astype(BF16) for value in streams])

    grads = [value.astype(F32) for value in to_chunks(cotangent)]
    outs = [None] * 6
    small = [None] * LAYERS
    for layer in reversed(range(LAYERS)):
        weight_qkv, weight_out, weight_up, weight_down = used[layer]
        sums = {}

        def add(name, value):
            sums[name] = value if name not in sums else sums[name] + value

        key_carry = value_carry = None
        for chunk in (1, 0):
            (
                unit,
                inverse,
                inputs,
                query,
                key,
                value,
                mixed,
                log_totals,
                unit_mid,
                inverse_mid,
                inputs_mid,
                hidden,
                active,
            ) = stored[layer][chunk]
            grad_stream = grads[chunk]
            grad_branch = grad_stream.astype(BF16)
            add("b_down", jnp.sum(grad_branch, axis=0, dtype=F32))
            branch_all = gather_rows(grad_branch)
            grad_active = dot_nt(branch_all, weight_down)
            grad_hidden = jax.vjp(gelu_tanh, hidden)[1](grad_active)[0].astype(BF16)
            add("w_down", dot_tn(active, branch_all))
            add("b_up", jnp.sum(grad_hidden, axis=0, dtype=F32))
            grad_normed_mid = scatter_rows(dot_nt(grad_hidden, weight_up).astype(BF16))
            add("w_up", dot_tn(inputs_mid, grad_hidden))
            add("gain_ffn", jnp.sum(grad_normed_mid * unit_mid, axis=0))
            add("shift_ffn", jnp.sum(grad_normed_mid, axis=0))
            grad_middle = grad_stream + norm_back(grad_normed_mid, unit_mid, inverse_mid, gain_ffn[layer])
            grad_attn = grad_middle.astype(BF16)
            add("b_out", jnp.sum(grad_attn, axis=0, dtype=F32))
            attn_all = gather_rows(grad_attn)
            grad_mixed = dot_nt(attn_all, weight_out).astype(BF16)
            add("w_out", dot_tn(mixed, attn_all))
            grad_query, grad_key, grad_value = attend_back(
                query, key, value, spot_sets[chunk], slopes, log_totals, grad_mixed
            )
            chunk_rows = query.shape[0]
            if chunk == 1:
                key_carry, value_carry = grad_key[:chunk_rows], grad_value[:chunk_rows]
                grad_key, grad_value = grad_key[chunk_rows:], grad_value[chunk_rows:]
            else:
                grad_key, grad_value = grad_key + key_carry, grad_value + value_carry
            grad_qkv = jnp.concatenate([grad_query, grad_key.astype(BF16), grad_value.astype(BF16)], 1)
            add("b_qkv", jnp.sum(grad_qkv, axis=0, dtype=F32))
            grad_normed = scatter_rows(dot_nt(grad_qkv, weight_qkv).astype(BF16))
            add("w_qkv", dot_tn(inputs, grad_qkv))
            add("gain_attn", jnp.sum(grad_normed * unit, axis=0))
            add("shift_attn", jnp.sum(grad_normed, axis=0))
            grads[chunk] = grad_middle + norm_back(grad_normed, unit, inverse, gain_attn[layer])

        for name, axes, members in (
            ("w_down", xy, ((5, 0, w_down.shape[2]),)),
            ("w_up", yx, ((4, 0, hidden_width),)),
            ("w_out", xy, ((3, 0, w_out.shape[2]),)),
            ("w_qkv", yx, tuple((index, index * head_width, head_width) for index in range(3))),
        ):
            piece = reduce_pair(reduce_plane(sums[name].astype(BF16), axes))
            pieces, spots = spread_weight(piece, axes)
            for index, column, width in members:
                outs[index] = store_pieces(pieces, spots, column, width, layer, outs[index])

        def spread(values, total):
            return lax.dynamic_update_slice_in_dim(
                jnp.zeros((total,), F32), values, shard * values.shape[0], 0
            )

        whole = head_width * 2 * across
        packed = jnp.concatenate(
            [sums[name] for name in ("gain_attn", "shift_attn", "b_out", "gain_ffn", "shift_ffn", "b_down")]
            + [
                spread(sums["b_qkv"][:head_width], whole),
                spread(sums["b_qkv"][2 * head_width :], whole),
                spread(sums["b_up"], b_up.shape[1]),
            ]
        )
        small[layer] = sum_small(packed.reshape(-1, 128)).reshape(-1)

    input_grad = from_chunks([value.astype(BF16) for value in grads])
    table = jnp.stack(small)
    wide = gain_attn.shape[1]
    shared = [table[:, index * wide : (index + 1) * wide] for index in range(6)]
    begin = 6 * wide
    whole = head_width * 2 * across
    grad_b_query = lax.dynamic_slice_in_dim(table[:, begin : begin + whole], home * head_width, head_width, 1)
    begin += whole
    grad_b_value = lax.dynamic_slice_in_dim(table[:, begin : begin + whole], home * head_width, head_width, 1)
    begin += whole
    grad_b_up = lax.dynamic_slice_in_dim(table[:, begin:], home * hidden_width, hidden_width, 1)
    return (
        activations_out,
        input_grad,
        shared[0],
        shared[1],
        outs[0],
        grad_b_query,
        outs[1],
        outs[2],
        grad_b_value,
        outs[3],
        shared[2],
        shared[3],
        shared[4],
        outs[4],
        grad_b_up,
        outs[5],
        shared[5],
    )


def solution(mesh):
    groups, parts = mesh.shape["dp"], mesh.shape["mp"]
    fine = Mesh(
        mesh.devices.reshape(2, groups // 4, 2, 2, parts // 2), ("ky", "kx", "c", "b", "r")
    )
    dp, mp = ("ky", "kx", "c"), ("b", "r")
    rows, whole = P(dp + mp, None), P()
    columns3, columns2, rows3 = P(None, None, mp), P(None, mp), P(None, mp, None)
    return jax.shard_map(
        local,
        mesh=fine,
        in_specs=(
            rows,
            P(dp, None),
            rows,
            whole,
            whole,
            columns3,
            columns2,
            columns3,
            columns3,
            columns2,
            rows3,
            whole,
            whole,
            whole,
            columns3,
            whole,
            rows3,
            whole,
        ),
        out_specs=(
            rows,
            rows,
            whole,
            whole,
            columns3,
            columns2,
            columns3,
            columns3,
            columns2,
            rows3,
            whole,
            whole,
            whole,
            columns3,
            columns2,
            rows3,
            whole,
        ),
        check_vma=False,
    )
```

```python
import functools

import jax
import jax.numpy as jnp
from jax import lax
from jax.experimental import pallas as pl
from jax.experimental.pallas import tpu as pltpu
from jax.sharding import Mesh
from jax.sharding import PartitionSpec as P

H = 8
HD = 128
LAYERS = 2
norm_eps = 1e-05
F32 = jnp.float32
BF16 = jnp.bfloat16
PLANE = ("c", "kx", "ky")
FETCH_ATTN = ("r", "0a", None, None), ("0c", "0d", "0e", "1a")
FETCH_FFN = (("s", 3), "0b", "0c", "0c2"), ("0e", "1a", "1c", "1c2")
COTANGENT = "1c"
ACTIVATIONS_OUT = "1f"
REDUCE_FFN = (
    ("0g", ("0h", 3), ("0j", 2), ("t1", 2), "t2", "t3", "t5"),
    ("1g", ("1h", 2), ("1i", 2), ("0f", 3), "0g", ("0g2", 2), "0j"),
)
REDUCE_ATTN = (
    ("0j", ("0j2", 2), "t2", "t3", "t4", "t5", "t6"),
    ("1j", "0f", ("0f2", 2), "0g", ("0h2", 2), ("0j2", 2), "t3"),
)
SUM_SMALL = ("t1", "t2", "t3", "t4", "t5", "t6")


def gelu_tanh(values):
    return jax.nn.gelu(values, approximate=True)


def norm_parts(stream):
    centred = stream - jnp.mean(stream, axis=-1, keepdims=True)
    inverse = lax.rsqrt(jnp.mean(centred * centred, axis=-1, keepdims=True) + norm_eps)
    return centred * inverse, inverse


def norm_back(grad_normed, unit_rows, inverse, gain):
    scaled = grad_normed * gain
    return inverse * (
        scaled
        - jnp.mean(scaled, axis=-1, keepdims=True)
        - unit_rows * jnp.mean(scaled * unit_rows, axis=-1, keepdims=True)
    )


def dot(left, right):
    return jnp.dot(left, right, preferred_element_type=F32)


def dot_nt(left, right):
    return jnp.einsum("ti,oi->to", left, right, preferred_element_type=F32)


def dot_tn(left, right):
    return jnp.einsum("ti,to->io", left, right, preferred_element_type=F32)


def after(value, other):
    return value if other is None else lax.optimization_barrier((value, other))[0]


def swap(value, axis):
    return lax.ppermute(value, axis, [(0, 1), (1, 0)])


def small_plane():
    return all(lax.axis_size(axis) == 2 for axis in PLANE)


def axis_order(axis):
    size = lax.axis_size(axis)
    if size == 2:
        return [lax.axis_index(axis), 1 - lax.axis_index(axis)]
    return list(range(size))


def gather_rows(rows, work, event):
    rows = work.at(event, rows)
    if lax.axis_size("r") == 2:
        across = work.at(event + "2", swap(rows, "r"))
        return jnp.concatenate([rows, across], 0)
    return work.at(event + "2", lax.all_gather(rows, "r", axis=0, tiled=True))


def scatter_rows(product, work, event):
    count = lax.axis_size("r")
    if count == 2:
        send = work.at(event, product(1, 2).astype(BF16))
        across = swap(send, "r")
        near = product(0, 1)
        return near + work.at(event + "2", across).astype(F32)
    partial = work.at(event, product(0, count).astype(BF16))
    across = lax.psum_scatter(partial, "r", scatter_dimension=0, tiled=True)
    return work.at(event + "2", across).astype(F32)


def to_chunks(value, token, at=lambda value: value):
    half = value.shape[0] // 2
    value = after(value, token)
    low, high = value[:half], value[half:]
    core, block = lax.axis_index("c"), lax.axis_index("b")
    first = jnp.where(block == 0, low, high)
    second = jnp.where(block == 0, high, low)
    first = at(first)
    first = lax.ppermute(first, ("c", "b"), [(0, 0), (1, 2), (2, 1), (3, 3)])
    second = lax.ppermute(second, ("c", "b"), [(0, 2), (1, 0), (2, 3), (3, 1)])
    yield [first, second]
    yield jnp.where(core == 0, jnp.concatenate([first, second], 0), jnp.concatenate([second, first], 0))


def from_chunks(rows, token):
    half = rows.shape[0] // 2
    rows = after(rows, token)
    early, late = rows[:half], rows[half:]
    core, block = lax.axis_index("c"), lax.axis_index("b")
    first = jnp.where(core == 0, early, late)
    second = jnp.where(core == 0, late, early)
    first = lax.ppermute(first, ("c", "b"), [(0, 0), (2, 1), (1, 2), (3, 3)])
    second = lax.ppermute(second, ("c", "b"), [(2, 0), (0, 1), (3, 2), (1, 3)])
    yield [first, second]
    yield jnp.where(block == 0, jnp.concatenate([first, second], 0), jnp.concatenate([second, first], 0))


def plane_count():
    return lax.axis_size("c") * lax.axis_size("kx") * lax.axis_size("ky")


def plane_place(c=None, x=None, y=None):
    c = lax.axis_index("c") if c is None else c
    x = lax.axis_index("kx") if x is None else x
    y = lax.axis_index("ky") if y is None else y
    return (c * lax.axis_size("kx") + x) * lax.axis_size("ky") + y


ORDERS = (("kx", "ky"), ("ky", "kx"))


def plane_places(ordered):
    spots = []
    for first, second in ORDERS:
        for c in axis_order("c"):
            for slow in axis_order(second):
                for fast in axis_order(first):
                    if ordered:
                        spots.append((c * 2 + fast) * 2 + slow)
                    else:
                        spots.append(plane_place(c, **{first[1]: fast, second[1]: slow}))
    return jnp.stack(spots).astype(jnp.int32)


def after_all(values, token):
    return [after(value, token) for value in values]


def spread_steps(work, pieces, token):
    token, span = token
    pieces = [piece[None] for piece in pieces]
    for stage in range(2):
        pieces = after_all(pieces, token)
        got = [swap(piece, order[stage]) for piece, order in zip(pieces, ORDERS)]
        work.expect(got, span)
        token, span = yield
        got = after_all(got, token)
        pieces = [jnp.concatenate(pair, 0) for pair in zip(pieces, got)]
        work.latest = pieces[0]
    return pieces, [swap(piece, "c") for piece in pieces]


class Background:
    def __init__(self):
        self.tasks = []
        self.waiting = []
        self.step = 0

    def advance(self, task, events, token):
        try:
            task.send(token)
            while events and (events[0] is None or events[0][0] is None):
                event = events.pop(0)
                task.send((None, event[1] if event else 1))
            self.tasks.append((task, events))
        except StopIteration:
            pass

    def add(self, task, events):
        self.advance(task, list(events), None)

    def expect(self, values, span=1):
        self.waiting += [(self.step + span, value) for value in values]

    def at(self, event, value):
        self.step += 1
        for due, result in self.waiting:
            if due <= self.step:
                value = after(value, result)
        self.waiting = [pair for pair in self.waiting if pair[0] > self.step]
        tasks, self.tasks = self.tasks, []
        for task, events in tasks:
            name, span = (events[0], 1) if isinstance(events[0], str) else events[0]
            if name == event:
                self.advance(task, events[1:], (value, span))
            else:
                self.tasks.append((task, events))
        return value


def sum_small(work, results, value):
    for axis in ("c", "kx", "ky", "r", "b"):
        token, span = yield
        value = after(value, token)
        if lax.axis_size(axis) == 2:
            got = swap(value, axis)
            work.expect([got], span)
            value = value + got
        else:
            value = lax.psum(value, axis)
    token, span = yield
    results["small"] = value


def cut_columns(value, parts):
    width = value.shape[1] // parts
    return jnp.concatenate([value[:, index * width : (index + 1) * width] for index in range(parts)], 0)


def cut_piece(weight, layer):
    size = weight.shape[1] // plane_count()
    return lax.dynamic_slice(weight, (layer, plane_place() * size, 0), (1, size, weight.shape[2]))[0]


def at_core(put, mine, beside):
    @pl.when(pl.program_id(0) < 4)
    def _():
        put(*mine)

    @pl.when(pl.program_id(0) >= 4)
    def _():
        put(*beside)


def place_attn_kernel(spots, kv, qo, kv_beside, qo_beside, query, key, value, out, to_query, to_kv, to_out):
    width = query.shape[2]
    rows = out.shape[1]

    def put(kv, qo):
        to_kv[:, :width] = key[0]
        to_kv[:, width : 2 * width] = kv[0, :, :width]
        to_kv[:, 2 * width : 3 * width] = value[0]
        to_kv[:, 3 * width :] = kv[0, :, width:]
        to_query[:, :width] = query[0]
        to_query[:, width:] = qo[0, :, :width]
        to_out[0] = out[0]
        for index in range(qo.shape[1] // rows):
            to_out[1, :, index * width : (index + 1) * width] = qo[
                0, index * rows : (index + 1) * rows, width:
            ]

    at_core(put, (kv, qo), (kv_beside, qo_beside))


def place_ffn_kernel(spots, up, down, up_beside, down_beside, to_up, to_down):
    def put(up, down):
        to_up[...] = up[0]
        to_down[...] = down[0]

    at_core(put, (up, down), (up_beside, down_beside))


def piece_specs(pieces):
    def spec(piece, core):
        return pl.BlockSpec((1,) + piece.shape[1:], lambda step, spots: (jnp.clip(step - core * 4, 0, 3), 0, 0))

    return [spec(piece, core) for core in range(2) for piece in pieces]


def row_spec(block, order, lead=0):
    if len(block) == 2:
        return pl.BlockSpec(block, lambda step, spots: (spots[order * 8 + step], 0))
    return pl.BlockSpec(block, lambda step, spots: (lead, spots[order * 8 + step], 0))


def place_call(kernel, mine, beside, owns, own_specs, outs, out_specs):
    size = sum(math_prod(shape) for shape in outs)
    return pl.pallas_call(
        kernel,
        out_shape=[jax.ShapeDtypeStruct(shape, BF16) for shape in outs],
        grid_spec=pltpu.PrefetchScalarGridSpec(
            num_scalar_prefetch=1,
            grid=(8,),
            in_specs=piece_specs(mine) + own_specs,
            out_specs=out_specs,
        ),
        compiler_params=pltpu.CompilerParams(vmem_limit_bytes=24 << 20),
        cost_estimate=pl.CostEstimate(flops=0, bytes_accessed=size * 4, transcendentals=0),
    )(plane_places(False), *mine, *beside, *owns)


def math_prod(shape):
    total = 1
    for size in shape:
        total *= size
    return total


def fetch_attn(work, used, layer, w_query, w_key, w_value, w_out):
    count = plane_count()
    depth, width = w_query.shape[1], w_query.shape[2]
    rows, out_rows = depth // count, width // count
    parts = depth // width
    kv = jnp.concatenate([cut_piece(w_key, layer), cut_piece(w_value, layer)], 1)
    qo = jnp.concatenate([cut_piece(w_query, layer), cut_columns(cut_piece(w_out, layer), parts)], 1)
    token, span = yield
    moved = swap(after(jnp.concatenate([kv, qo], 1), token), "b")
    work.expect([moved], span)
    pieces = [moved[:, : 2 * width], moved[:, 2 * width :]]
    token = yield
    if small_plane() and out_rows % 16 == 0:
        mine, beside = yield from spread_steps(work, pieces, token)
        query, kv, out = place_call(
            place_attn_kernel,
            mine,
            beside,
            (w_query, w_key, w_value, w_out),
            [row_spec((1, rows, width), order, layer) for order in (1, 0, 0)]
            + [row_spec((1, out_rows, depth), 1, layer)],
            ((depth, 2 * width), (depth, 4 * width), (2, width, depth)),
            [
                row_spec((rows, 2 * width), 1),
                row_spec((rows, 4 * width), 0),
                row_spec((2, out_rows, depth), 1),
            ],
        )
        used["attn", layer] = (query, kv, out.reshape(2 * width, depth))
        return
    packed = jnp.concatenate([lax.all_gather(piece, PLANE, axis=0) for piece in pieces], 2)
    kv, qo = packed[:, :, : 2 * width], packed[:, :, 2 * width :]
    out = qo[:, :, width:].reshape(count, parts, out_rows, width).transpose(0, 2, 1, 3).reshape(width, depth)
    kv = kv.reshape(depth, 2 * width)
    query = jnp.concatenate([w_query[layer], qo[:, :, :width].reshape(depth, width)], 1)
    kv = jnp.concatenate([w_key[layer], kv[:, :width], w_value[layer], kv[:, width:]], 1)
    used["attn", layer] = (query, kv, jnp.concatenate([w_out[layer], out], 0))


def fetch_ffn(work, used, layer, w_up, w_down):
    count = plane_count()
    depth, width = w_up.shape[1], w_up.shape[2]
    rows, down_rows = depth // count, width // count
    pieces = [cut_piece(weight, layer) for weight in (w_up, w_down)]
    token, span = yield
    if width == depth:
        moved = swap(after(jnp.concatenate(pieces, 1), token), "b")
        pieces = [moved[:, :width], moved[:, width:]]
    else:
        pieces = [swap(piece, "b") for piece in after_all(pieces, token)]
    work.expect(pieces, span)
    token = yield
    if small_plane() and width == depth:
        mine, beside = yield from spread_steps(work, pieces, token)
        used["ffn", layer] = place_call(
            place_ffn_kernel,
            mine,
            beside,
            (),
            [],
            ((depth, width), (width, depth)),
            [row_spec((rows, width), 0), row_spec((down_rows, depth), 1)],
        )
        return
    used["ffn", layer] = [lax.all_gather(piece, PLANE, axis=0, tiled=True) for piece in pieces]


def store_kernel(layout, arrays, given, spots, *refs):
    outs = refs[2 * arrays + given :]

    def put(*pieces):
        for out, (half, begin, width, turn) in zip(outs, layout):
            block = pieces[half][0, :, begin : begin + width].astype(F32)
            out[0] = block.T if turn else block

    at_core(put, refs[:arrays], refs[arrays : 2 * arrays])


def reduce_weights(work, results, name, layer, halves_of, layout):
    depth = halves_of[0][0][0].shape[1]
    widths = [[right.shape[1] // 2 for _, right in pairs] for pairs in halves_of]

    def side(value, half, which):
        parts, begin = [], 0
        for width in widths[half]:
            parts.append(value[:, begin + which * width : begin + (which + 1) * width])
            begin += 2 * width
        return jnp.concatenate(parts, 1)

    def grads_of(place, size, token):
        return [
            jnp.concatenate(
                [
                    dot_tn(lax.dynamic_slice_in_dim(left, place * size, size, 1), right)
                    for left, right in [(after(left, token), right) for left, right in pairs]
                ],
                1,
            ).astype(BF16)
            for pairs in halves_of
        ]

    token, span = yield
    if small_plane():
        core = lax.axis_index("c")
        size = depth // 2
        beside = [swap(grad, "c") for grad in grads_of(1 - core, size, token)]
        kept = grads_of(core, size, token)
        work.expect(kept + beside, span)

        def cut(half, other):
            index = lax.axis_index(ORDERS[half][0])
            begin = (1 - index if other else index) * (size // 2)
            return sum(
                lax.dynamic_slice_in_dim(value[half], begin, size // 2, 0).astype(F32) for value in (kept, beside)
            )

        token, span = yield
        kept, beside = after_all(kept, token), after_all(beside, token)
        got = [swap(cut(half, True).astype(BF16), ORDERS[half][0]) for half in range(2)]
        work.expect(got, span)
        near = [cut(half, False) for half in range(2)]
        token, span = yield
        size = size // 4
        totals = [(value + part.astype(F32)).astype(BF16) for value, part in zip(near, after_all(got, token))]
        work.latest = totals[0]
        index = [lax.axis_index(order[1]) for order in ORDERS]
        got = [
            swap(lax.dynamic_slice_in_dim(value, (1 - i) * size, size, 0), order[1])
            for value, i, order in zip(totals, index, ORDERS)
        ]
        work.expect(got, span)
        near = [lax.dynamic_slice_in_dim(value, i * size, size, 0) for value, i in zip(totals, index)]
        token, span = yield
        totals = [
            (value.astype(F32) + part.astype(F32)).astype(BF16)
            for value, part in zip(near, after_all(got, token))
        ]
        work.latest = totals[0]
    else:
        totals = [
            lax.psum_scatter(grad, PLANE, scatter_dimension=0, tiled=True) for grad in grads_of(0, depth, token)
        ]
        token, span = yield
    other = jnp.concatenate([side(value, half, 1) for half, value in enumerate(totals)], 1)
    got = swap(after(other, token), "b")
    work.expect([got], span)
    token = yield
    other = after(got, token[0])
    pieces, begin = [], 0
    for half, value in enumerate(totals):
        own = side(value, half, 0)
        part = other[:, begin : begin + own.shape[1]]
        begin += own.shape[1]
        pieces.append((own.astype(F32) + part.astype(F32)).astype(BF16))
    work.latest = pieces[0]
    rows = depth // plane_count()
    shapes = [(LAYERS, w, depth) if turn else (LAYERS, depth, w) for _, _, w, turn in layout]
    before = results.get(name)
    if not (small_plane() and rows % 128 == 0):
        stored = []
        for index, (half, begin, width, turn) in enumerate(layout):
            block = lax.all_gather(pieces[half][:, begin : begin + width], PLANE, axis=0, tiled=True)
            block = block.astype(F32)
            block = block.T if turn else block
            base = jnp.zeros(shapes[index], F32) if before is None else before[index]
            stored.append(base.at[layer].set(block))
        results[name] = stored
        return
    mine, beside = yield from spread_steps(work, pieces, token)
    given = list(before or [])
    size = sum(math_prod(shape) for shape in shapes) // LAYERS

    def out_spec(half, width, turn):
        if turn:
            return pl.BlockSpec((1, width, rows), lambda step, spots: (layer, 0, spots[half * 8 + step]))
        return row_spec((1, rows, width), half, layer)

    results[name] = pl.pallas_call(
        functools.partial(store_kernel, layout, len(mine), len(given)),
        out_shape=[jax.ShapeDtypeStruct(shape, F32) for shape in shapes],
        grid_spec=pltpu.PrefetchScalarGridSpec(
            num_scalar_prefetch=1,
            grid=(8,),
            in_specs=piece_specs(mine) + [pl.BlockSpec(memory_space=pl.ANY)] * len(given),
            out_specs=[out_spec(half, width, turn) for half, _, width, turn in layout],
        ),
        input_output_aliases={1 + len(mine + beside) + index: index for index in range(len(given))},
        compiler_params=pltpu.CompilerParams(vmem_limit_bytes=24 << 20),
        cost_estimate=pl.CostEstimate(flops=0, bytes_accessed=size * 6, transcendentals=0),
    )(plane_places(True), *mine, *beside, *given)
    work.expect(list(results[name]))


def halves(ref, size, columns, odd):
    count = ref.shape[0] // size
    return jnp.concatenate(
        [ref[index * size : (index + 1) * size, columns] for index in range(odd, count, 2)], 0
    )


def both_cores(mine, beside, size, columns, odd):
    return jnp.concatenate([halves(mine, size, columns, odd), halves(beside, size, columns, odd)], 0)


def tile_scores(query, keys, at_query, at_keys, slope):
    scores = lax.dot_general(query, keys, (((1,), (1,)), ((), ())), preferred_element_type=F32)
    place, start = at_query
    scores = scores * HD ** (-0.5) - slope * (place - at_keys)
    return jnp.where((at_keys <= place) & (at_keys >= start), scores, -1e30)


def attend_kernel(size, slopes, at_rows, at_keys, query, mine, beside, mixed, log_totals):
    heads = query.shape[1] // HD
    for head in range(heads):
        columns = slice(head * HD, (head + 1) * HD)
        value_columns = slice((heads + head) * HD, (heads + head + 1) * HD)
        keys = [both_cores(mine, beside, size, columns, odd) for odd in range(2)]
        values = [both_cores(mine, beside, size, value_columns, odd) for odd in range(2)]
        for odd in range(2):
            key_rows = keys[0] if odd == 0 else jnp.concatenate(keys, 0)
            value_rows = values[0] if odd == 0 else jnp.concatenate(values, 0)
            spots = at_keys[:, : key_rows.shape[0]]
            scores = tile_scores(
                halves(query, size, columns, odd),
                key_rows,
                (at_rows[:, 2 * odd : 2 * odd + 1], at_rows[:, 2 * odd + 1 : 2 * odd + 2]),
                spots,
                slopes[head],
            )
            row_max = jnp.max(scores, axis=-1, keepdims=True)
            weights = jnp.exp(scores - row_max)
            totals = jnp.sum(weights, axis=-1, keepdims=True)
            probabilities = (weights * (1.0 / totals)).astype(BF16)
            result = jnp.dot(probabilities, value_rows, preferred_element_type=F32).astype(BF16)
            logs = row_max + jnp.log(totals)
            for index in range(result.shape[0] // size):
                rows = slice((2 * index + odd) * size, (2 * index + odd + 1) * size)
                mixed[rows, columns] = result[index * size : (index + 1) * size]
                log_totals[rows, head : head + 1] = logs[index * size : (index + 1) * size]


def attend_back_kernel(
    size, slopes, at_rows, at_keys, query, mine, beside, log_totals, grad, to_query, to_mine, to_beside
):
    heads = query.shape[1] // HD
    scale = HD ** (-0.5)
    for head in range(heads):
        columns = slice(head * HD, (head + 1) * HD)
        value_columns = slice((heads + head) * HD, (heads + head + 1) * HD)
        one = slice(head, head + 1)
        keys = [both_cores(mine, beside, size, columns, odd) for odd in range(2)]
        values = [both_cores(mine, beside, size, value_columns, odd) for odd in range(2)]
        key_total = value_total = None
        for odd in (1, 0):
            key_rows = keys[0] if odd == 0 else jnp.concatenate(keys, 0)
            value_rows = values[0] if odd == 0 else jnp.concatenate(values, 0)
            query_rows = halves(query, size, columns, odd)
            grad_rows = halves(grad, size, columns, odd)
            scores = tile_scores(
                query_rows,
                key_rows,
                (at_rows[:, 2 * odd : 2 * odd + 1], at_rows[:, 2 * odd + 1 : 2 * odd + 2]),
                at_keys[:, : key_rows.shape[0]],
                slopes[head],
            )
            probabilities = jnp.exp(scores - halves(log_totals, size, one, odd))
            grad_probs = lax.dot_general(
                grad_rows, value_rows, (((1,), (1,)), ((), ())), preferred_element_type=F32
            )
            centre = jnp.sum(grad_probs * probabilities, axis=-1, keepdims=True)
            grad_scores = (probabilities * (grad_probs - centre)).astype(BF16)
            grad_value = lax.dot_general(
                probabilities.astype(BF16), grad_rows, (((0,), (0,)), ((), ())), preferred_element_type=F32
            )
            grad_query = jnp.dot(grad_scores, key_rows, preferred_element_type=F32) * scale
            grad_key = (
                lax.dot_general(grad_scores, query_rows, (((0,), (0,)), ((), ())), preferred_element_type=F32)
                * scale
            )
            grad_query = grad_query.astype(BF16)
            for index in range(grad_query.shape[0] // size):
                rows = slice((2 * index + odd) * size, (2 * index + odd + 1) * size)
                to_query[rows, columns] = grad_query[index * size : (index + 1) * size]
            if odd == 1:
                early = keys[0].shape[0]
                results = [(grad_key[early:], grad_value[early:], 1)]
                key_total, value_total = grad_key[:early], grad_value[:early]
            else:
                results = [(grad_key + key_total, grad_value + value_total, 0)]
            for grad_key, grad_value, part in results:
                blocks = grad_key.shape[0] // size // 2
                for index in range(blocks):
                    rows = slice((2 * index + part) * size, (2 * index + part + 1) * size)
                    near = slice(index * size, (index + 1) * size)
                    far = slice((blocks + index) * size, (blocks + index + 1) * size)
                    to_mine[rows, columns] = grad_key[near]
                    to_mine[rows, value_columns] = grad_value[near]
                    to_beside[rows, columns] = grad_key[far].astype(BF16)
                    to_beside[rows, value_columns] = grad_value[far].astype(BF16)


def attention_cost(query, products):
    elements = query.shape[0] * query.shape[0] * 3 // 2 * (query.shape[1] // HD)
    return pl.CostEstimate(
        flops=elements * HD * 2 * products, bytes_accessed=query.size * 16, transcendentals=elements
    )


def attention_specs(count):
    return [pl.BlockSpec(memory_space=pltpu.SMEM)] + [pl.BlockSpec(memory_space=pltpu.VMEM)] * count


def attend(query, mine, beside, info):
    slopes, at_rows, at_keys, size = info
    return pl.pallas_call(
        functools.partial(attend_kernel, size),
        out_shape=[
            jax.ShapeDtypeStruct(query.shape, BF16),
            jax.ShapeDtypeStruct((query.shape[0], query.shape[1] // HD), F32),
        ],
        in_specs=attention_specs(5),
        out_specs=[pl.BlockSpec(memory_space=pltpu.VMEM)] * 2,
        compiler_params=pltpu.CompilerParams(vmem_limit_bytes=48 << 20),
        cost_estimate=attention_cost(query, 2),
    )(slopes, at_rows, at_keys, query, mine, beside)


def attend_back(query, mine, beside, log_totals, grad_mixed, info):
    slopes, at_rows, at_keys, size = info
    return pl.pallas_call(
        functools.partial(attend_back_kernel, size),
        out_shape=[
            jax.ShapeDtypeStruct(query.shape, BF16),
            jax.ShapeDtypeStruct(mine.shape, F32),
            jax.ShapeDtypeStruct(mine.shape, BF16),
        ],
        in_specs=attention_specs(7),
        out_specs=[pl.BlockSpec(memory_space=pltpu.VMEM)] * 3,
        compiler_params=pltpu.CompilerParams(vmem_limit_bytes=48 << 20),
        cost_estimate=attention_cost(query, 5),
    )(slopes, at_rows, at_keys, query, mine, beside, log_totals, grad_mixed)


def attention_info(lengths, slopes, size):
    block, core = lax.axis_index("b"), lax.axis_index("c")
    ends = jnp.cumsum(jnp.where(core == block, lengths, swap(lengths, "c")))
    across = lax.axis_size("r")
    steps = jnp.arange(size, dtype=jnp.int32)

    def spots(which, odd):
        return jnp.concatenate([((odd * across + place) * 2 + which) * size + steps for place in axis_order("r")])

    columns, keys = [], []
    for odd in range(2):
        place = spots(core, odd)
        start = jnp.max(jnp.where(place[:, None] >= ends[None, :], ends[None, :], 0), axis=1)
        columns += [place, start]
        keys += [spots(which, odd) for which in axis_order("c")]
    at_rows = jnp.stack(columns, 1).astype(F32)
    at_keys = jnp.concatenate(keys)[None, :].astype(F32)
    return slopes, at_rows, at_keys, size


def local(
    activations,
    lengths,
    cotangent,
    gain_attn,
    shift_attn,
    w_query,
    b_query,
    w_key,
    w_value,
    b_value,
    w_out,
    b_out,
    gain_ffn,
    shift_ffn,
    w_up,
    b_up,
    w_down,
    b_down,
):
    block, place = lax.axis_index("b"), lax.axis_index("r")
    across = lax.axis_size("r")
    shards = [block * across + place, (1 - block) * across + place]
    head_width = w_query.shape[2]
    head_count = head_width // HD
    hidden_width = w_up.shape[2]

    head_ids = jnp.concatenate(
        [shard * head_count + jnp.arange(head_count, dtype=jnp.int32) for shard in shards]
    ).astype(F32)
    slopes = 2.0 ** (-8.0 * (head_ids + 1.0) / H)
    info = attention_info(lengths[0], slopes, activations.shape[0] // 2)

    bias_own = jnp.concatenate([b_query, b_value], 1)
    bias_other = swap(bias_own, "b")

    used, results = {}, {}
    work = Background()
    for layer in range(LAYERS):
        work.add(
            fetch_attn(work, used, layer, w_query, w_key, w_value, w_out),
            FETCH_ATTN[layer],
        )
        work.add(fetch_ffn(work, used, layer, w_up, w_down), FETCH_FFN[layer])

    def move(name, steps, value):
        token, span = yield
        steps = steps(value, token)
        work.expect(next(steps), span)
        results[name] = next(steps)

    moving = to_chunks(activations, None, lambda value: work.at("r", value))
    next(moving)
    stream = work.at("s", next(moving).astype(F32))
    work.add(move("cotangent", to_chunks, cotangent), (COTANGENT,))

    def rows_of(array, first, last):
        size = array.shape[0] // across
        return array[first * size : last * size]

    stored = []
    zero = jnp.zeros((2 * head_width,), F32)
    for layer in range(LAYERS):
        bias_query = jnp.concatenate([bias_own[layer, :head_width], bias_other[layer, :head_width]])
        bias_kv = jnp.concatenate([zero, bias_own[layer, head_width:], bias_other[layer, head_width:]])
        bias_up = [
            lax.dynamic_slice_in_dim(b_up[layer], shard * hidden_width, hidden_width, 0) for shard in shards
        ]
        unit, inverse = norm_parts(stream)
        inputs = gather_rows((unit * gain_attn[layer] + shift_attn[layer]).astype(BF16), work, str(layer) + "a")
        weight_query, weight_kv, weight_out = used["attn", layer]
        mine = (dot(inputs, weight_kv) + bias_kv).astype(BF16)
        mine = work.at(str(layer) + "b", mine)
        beside = swap(mine, "c")
        query = (dot(inputs, weight_query) + bias_query).astype(BF16)
        mixed, log_totals = attend(query, mine, beside, info)
        middle = stream + (
            scatter_rows(lambda first, last: dot(rows_of(mixed, first, last), weight_out), work, str(layer) + "c") + b_out[layer]
        )
        unit_mid, inverse_mid = norm_parts(middle)
        inputs_mid = gather_rows((unit_mid * gain_ffn[layer] + shift_ffn[layer]).astype(BF16), work, str(layer) + "d")
        ups, downs = zip((w_up[layer], w_down[layer]), used["ffn", layer])
        hidden = [dot(inputs_mid, up) + bias for up, bias in zip(ups, bias_up)]
        active = [gelu_tanh(value).astype(BF16) for value in hidden]
        stream = middle + (
            scatter_rows(lambda first, last: sum(dot(rows_of(value, first, last), down) for value, down in zip(active, downs)),
                work, str(layer) + "e") + b_down[layer]
        )
        stored.append(
            (
                unit,
                inverse,
                inputs,
                query,
                mine,
                beside,
                mixed,
                log_totals,
                unit_mid,
                inverse_mid,
                inputs_mid,
                hidden,
                active,
            )
        )
    work.add(move("activations_out", from_chunks, stream.astype(BF16)), (ACTIVATIONS_OUT,))
    grad_stream = results["cotangent"].astype(F32)
    small = {}
    for layer in reversed(range(LAYERS)):
        weight_query, weight_kv, weight_out = used["attn", layer]
        ups, downs = zip((w_up[layer], w_down[layer]), used["ffn", layer])
        (
            unit,
            inverse,
            inputs,
            query,
            mine,
            beside,
            mixed,
            log_totals,
            unit_mid,
            inverse_mid,
            inputs_mid,
            hidden,
            active,
        ) = stored[layer]
        grad_branch = grad_stream.astype(BF16)
        grad_b_down = jnp.sum(grad_branch, axis=0, dtype=F32)
        branch_all = gather_rows(grad_branch, work, str(layer) + "f")
        grad_hidden = [
            jax.vjp(gelu_tanh, value)[1](dot_nt(branch_all, down))[0].astype(BF16)
            for value, down in zip(hidden, downs)
        ]
        work.add(
            reduce_weights(
                work,
                results,
                "ffn",
                layer,
                ([(inputs_mid, jnp.concatenate(grad_hidden, 1))], [(branch_all, jnp.concatenate(active, 1))]),
                ((0, 0, hidden_width, False), (1, 0, hidden_width, True)),
            ),
            REDUCE_FFN[layer],
        )
        grad_normed_mid = scatter_rows(
            lambda first, last: sum(dot_nt(rows_of(value, first, last), up) for value, up in zip(grad_hidden, ups)),
            work,
            str(layer) + "g",
        )
        grad_b_up = jnp.concatenate([jnp.sum(value, axis=0, dtype=F32) for value in grad_hidden])
        grad_gain_ffn = jnp.sum(grad_normed_mid * unit_mid, axis=0)
        grad_shift_ffn = jnp.sum(grad_normed_mid, axis=0)
        grad_middle = grad_stream + norm_back(grad_normed_mid, unit_mid, inverse_mid, gain_ffn[layer])
        grad_attn = grad_middle.astype(BF16)
        grad_b_out = jnp.sum(grad_attn, axis=0, dtype=F32)
        attn_all = gather_rows(grad_attn, work, str(layer) + "h")
        grad_mixed = dot_nt(attn_all, weight_out).astype(BF16)
        grad_query, grad_mine, grad_beside = attend_back(query, mine, beside, log_totals, grad_mixed, info)
        grad_beside = work.at(str(layer) + "i", grad_beside)
        grad_kv = (grad_mine + swap(grad_beside, "c").astype(F32)).astype(BF16)
        work.add(
            reduce_weights(
                work,
                results,
                "attn",
                layer,
                (
                    [(inputs, grad_kv[:, : 2 * head_width]), (inputs, grad_kv[:, 2 * head_width :])],
                    [(inputs, grad_query), (attn_all, mixed)],
                ),
                (
                    (1, 0, head_width, False),
                    (0, 0, head_width, False),
                    (0, head_width, head_width, False),
                    (1, head_width, head_width, True),
                ),
            ),
            REDUCE_ATTN[layer],
        )
        grad_normed = scatter_rows(
            lambda first, last: dot_nt(rows_of(grad_query, first, last), weight_query)
            + dot_nt(rows_of(grad_kv, first, last), weight_kv),
            work,
            str(layer) + "j",
        )
        grad_b_query = jnp.sum(grad_query, axis=0, dtype=F32)
        grad_b_value = jnp.sum(grad_kv[:, 2 * head_width :], axis=0, dtype=F32)
        grads_in = grad_normed
        grad_gain_attn = jnp.sum(grad_normed * unit, axis=0)
        grad_shift_attn = jnp.sum(grad_normed, axis=0)
        grad_stream = grad_middle + norm_back(grad_normed, unit, inverse, gain_attn[layer])

        def spread(values, total):
            width = values.shape[0] // 2
            result = jnp.zeros((total,), F32)
            for index, shard in enumerate(shards):
                result = lax.dynamic_update_slice_in_dim(
                    result, values[index * width : (index + 1) * width], shard * width, 0
                )
            return result

        whole = head_width * 2 * across
        packed = jnp.concatenate(
            [
                grad_gain_attn,
                grad_shift_attn,
                grad_b_out,
                grad_gain_ffn,
                grad_shift_ffn,
                grad_b_down,
                spread(grad_b_query, whole),
                spread(grad_b_value, whole),
                spread(grad_b_up, b_up.shape[1]),
            ]
        )
        small[layer] = packed.reshape(-1, 128)

    work.add(sum_small(work, results, jnp.stack([small[layer] for layer in range(LAYERS)])), SUM_SMALL)
    work.at("t1", grads_in)
    leaving = from_chunks(grad_stream.astype(BF16), None)
    next(leaving)
    input_grad = next(leaving)
    for step in range(2, 7):
        work.at("t" + str(step), work.latest)
    assert not work.tasks
    attn_outs, ffn_outs = results["attn"], results["ffn"]
    table = results["small"].reshape(LAYERS, -1)
    wide = gain_attn.shape[1]
    shared = [table[:, index * wide : (index + 1) * wide] for index in range(6)]
    begin = 6 * wide
    whole = head_width * 2 * across
    home = shards[0]
    all_b_query = lax.dynamic_slice_in_dim(table[:, begin : begin + whole], home * head_width, head_width, 1)
    begin += whole
    all_b_value = lax.dynamic_slice_in_dim(table[:, begin : begin + whole], home * head_width, head_width, 1)
    begin += whole
    all_b_up = lax.dynamic_slice_in_dim(table[:, begin:], home * hidden_width, hidden_width, 1)
    return (
        results["activations_out"],
        input_grad,
        shared[0],
        shared[1],
        attn_outs[0],
        all_b_query,
        attn_outs[1],
        attn_outs[2],
        all_b_value,
        attn_outs[3],
        shared[2],
        shared[3],
        shared[4],
        ffn_outs[0],
        all_b_up,
        ffn_outs[1],
        shared[5],
    )


def solution(mesh):
    groups, parts = mesh.shape["dp"], mesh.shape["mp"]
    fine = Mesh(
        mesh.devices.reshape(2, groups // 4, 2, 2, parts // 2), ("ky", "kx", "c", "b", "r")
    )
    dp, mp = ("ky", "kx", "c"), ("b", "r")
    rows, whole = P(dp + mp, None), P()
    columns3, columns2, rows3 = P(None, None, mp), P(None, mp), P(None, mp, None)
    return jax.shard_map(
        local,
        mesh=fine,
        in_specs=(
            rows,
            P(dp, None),
            rows,
            whole,
            whole,
            columns3,
            columns2,
            columns3,
            columns3,
            columns2,
            rows3,
            whole,
            whole,
            whole,
            columns3,
            whole,
            rows3,
            whole,
        ),
        out_specs=(
            rows,
            rows,
            whole,
            whole,
            columns3,
            columns2,
            columns3,
            columns3,
            columns2,
            rows3,
            whole,
            whole,
            whole,
            columns3,
            columns2,
            rows3,
            whole,
        ),
        check_vma=False,
    )
```

```python
import functools

import jax
import jax.numpy as jnp
from jax import lax
from jax.experimental import pallas as pl
from jax.experimental.pallas import tpu as pltpu
from jax.sharding import Mesh
from jax.sharding import PartitionSpec as P

H = 8
HD = 128
LAYERS = 2
norm_eps = 1e-05
F32 = jnp.float32
BF16 = jnp.bfloat16
PLANE = ("c", "kx", "ky")
FETCH_ATTN = ("r", "0a", None, None), ("0c", "0d", "0e", "1a")
FETCH_FFN = (("s", 3), "0b", "0c", "0d", "0d2"), ("0e", (None, 1), "1a", "1c", "1c2")
COTANGENT = "1c"
ACTIVATIONS_OUT = "1f"
REDUCE_FFN = (
    ("0g", ("0h", 3), ("0j", 2), ("t1", 2), "t2", "t3", "t5"),
    ("1g", ("1h", 2), ("1i", 2), ("0f", 3), "0g", ("0g2", 2), "0j"),
)
REDUCE_ATTN = (
    ("0j", ("0j2", 2), "t2", "t3", "t4", "t5", "t6"),
    ("1j", "0f", ("0f2", 2), "0g", ("0h2", 2), ("0j2", 2), "t3"),
)
SUM_SMALL = ("t1", "t2", "t3", "t4", "t5", "t6")


def gelu_tanh(values):
    return jax.nn.gelu(values, approximate=True)


def norm_parts(stream):
    centred = stream - jnp.mean(stream, axis=-1, keepdims=True)
    inverse = lax.rsqrt(jnp.mean(centred * centred, axis=-1, keepdims=True) + norm_eps)
    return centred * inverse, inverse


def norm_back(grad_normed, unit_rows, inverse, gain):
    scaled = grad_normed * gain
    return inverse * (
        scaled
        - jnp.mean(scaled, axis=-1, keepdims=True)
        - unit_rows * jnp.mean(scaled * unit_rows, axis=-1, keepdims=True)
    )


def dot(left, right):
    return jnp.dot(left, right, preferred_element_type=F32)


def dot_nt(left, right):
    return jnp.einsum("ti,oi->to", left, right, preferred_element_type=F32)


def dot_tn(left, right):
    return jnp.einsum("ti,to->io", left, right, preferred_element_type=F32)


def after(value, other):
    return value if other is None else lax.optimization_barrier((value, other))[0]


def swap(value, axis):
    return lax.ppermute(value, axis, [(0, 1), (1, 0)])


def small_plane():
    return all(lax.axis_size(axis) == 2 for axis in PLANE)


def axis_order(axis):
    size = lax.axis_size(axis)
    if size == 2:
        return [lax.axis_index(axis), 1 - lax.axis_index(axis)]
    return list(range(size))


def gather_rows(rows, work, event):
    rows = work.at(event, rows)
    if lax.axis_size("r") == 2:
        across = work.at(event + "2", swap(rows, "r"))
        return jnp.concatenate([rows, across], 0)
    return work.at(event + "2", lax.all_gather(rows, "r", axis=0, tiled=True))


def scatter_rows(product, work, event):
    count = lax.axis_size("r")
    if count == 2:
        send = work.at(event, product(1, 2).astype(BF16))
        across = swap(send, "r")
        near = product(0, 1)
        return near + work.at(event + "2", across).astype(F32)
    partial = work.at(event, product(0, count).astype(BF16))
    across = lax.psum_scatter(partial, "r", scatter_dimension=0, tiled=True)
    return work.at(event + "2", across).astype(F32)


def to_chunks(value, token, at=lambda value: value):
    half = value.shape[0] // 2
    value = after(value, token)
    low, high = value[:half], value[half:]
    core, block = lax.axis_index("c"), lax.axis_index("b")
    first = jnp.where(block == 0, low, high)
    second = jnp.where(block == 0, high, low)
    first = at(first)
    first = lax.ppermute(first, ("c", "b"), [(0, 0), (1, 2), (2, 1), (3, 3)])
    second = lax.ppermute(second, ("c", "b"), [(0, 2), (1, 0), (2, 3), (3, 1)])
    yield [first, second]
    yield jnp.where(core == 0, jnp.concatenate([first, second], 0), jnp.concatenate([second, first], 0))


def from_chunks(rows, token):
    half = rows.shape[0] // 2
    rows = after(rows, token)
    early, late = rows[:half], rows[half:]
    core, block = lax.axis_index("c"), lax.axis_index("b")
    first = jnp.where(core == 0, early, late)
    second = jnp.where(core == 0, late, early)
    first = lax.ppermute(first, ("c", "b"), [(0, 0), (2, 1), (1, 2), (3, 3)])
    second = lax.ppermute(second, ("c", "b"), [(2, 0), (0, 1), (3, 2), (1, 3)])
    yield [first, second]
    yield jnp.where(block == 0, jnp.concatenate([first, second], 0), jnp.concatenate([second, first], 0))


def plane_count():
    return lax.axis_size("c") * lax.axis_size("kx") * lax.axis_size("ky")


def plane_place(c=None, x=None, y=None):
    c = lax.axis_index("c") if c is None else c
    x = lax.axis_index("kx") if x is None else x
    y = lax.axis_index("ky") if y is None else y
    return (c * lax.axis_size("kx") + x) * lax.axis_size("ky") + y


ORDERS = (("kx", "ky"), ("ky", "kx"))


def plane_places(ordered):
    spots = []
    for first, second in ORDERS:
        for c in axis_order("c"):
            for slow in axis_order(second):
                for fast in axis_order(first):
                    if ordered:
                        spots.append((c * 2 + fast) * 2 + slow)
                    else:
                        spots.append(plane_place(c, **{first[1]: fast, second[1]: slow}))
    return jnp.stack(spots).astype(jnp.int32)


def after_all(values, token):
    return [after(value, token) for value in values]


def spread_steps(work, pieces, token):
    token, span = token
    pieces = [piece[None] for piece in pieces]
    for stage in range(2):
        pieces = after_all(pieces, token)
        got = [swap(piece, order[stage]) for piece, order in zip(pieces, ORDERS)]
        work.expect(got, span)
        token, span = yield
        got = after_all(got, token)
        pieces = [jnp.concatenate(pair, 0) for pair in zip(pieces, got)]
        work.latest = pieces[0]
    return pieces, [swap(piece, "c") for piece in pieces]


class Background:
    def __init__(self):
        self.tasks = []
        self.waiting = []
        self.step = 0

    def advance(self, task, events, token):
        try:
            task.send(token)
            while events and (events[0] is None or events[0][0] is None):
                event = events.pop(0)
                task.send((None, event[1] if event else 1))
            self.tasks.append((task, events))
        except StopIteration:
            pass

    def add(self, task, events):
        self.advance(task, list(events), None)

    def expect(self, values, span=1):
        self.waiting += [(self.step + span, value) for value in values]

    def at(self, event, value):
        self.step += 1
        for due, result in self.waiting:
            if due <= self.step:
                value = after(value, result)
        self.waiting = [pair for pair in self.waiting if pair[0] > self.step]
        tasks, self.tasks = self.tasks, []
        for task, events in tasks:
            name, span = (events[0], 1) if isinstance(events[0], str) else events[0]
            if name == event:
                self.advance(task, events[1:], (value, span))
            else:
                self.tasks.append((task, events))
        return value


def sum_small(work, results, value):
    for axis in ("c", "kx", "ky", "r", "b"):
        token, span = yield
        value = after(value, token)
        if lax.axis_size(axis) == 2:
            got = swap(value, axis)
            work.expect([got], span)
            value = value + got
        else:
            value = lax.psum(value, axis)
    token, span = yield
    results["small"] = value


def cut_columns(value, parts):
    width = value.shape[1] // parts
    return jnp.concatenate([value[:, index * width : (index + 1) * width] for index in range(parts)], 0)


def cut_piece(weight, layer):
    size = weight.shape[1] // plane_count()
    return lax.dynamic_slice(weight, (layer, plane_place() * size, 0), (1, size, weight.shape[2]))[0]


def at_core(put, mine, beside):
    @pl.when(pl.program_id(0) < 4)
    def _():
        put(*mine)

    @pl.when(pl.program_id(0) >= 4)
    def _():
        put(*beside)


def place_attn_kernel(spots, kv, qo, kv_beside, qo_beside, query, key, value, out, to_query, to_kv, to_out):
    width = query.shape[2]
    rows = out.shape[1]

    def put(kv, qo):
        to_kv[:, :width] = key[0]
        to_kv[:, width : 2 * width] = kv[0, :, :width]
        to_kv[:, 2 * width : 3 * width] = value[0]
        to_kv[:, 3 * width :] = kv[0, :, width:]
        to_query[:, :width] = query[0]
        to_query[:, width:] = qo[0, :, :width]
        to_out[0] = out[0]
        for index in range(qo.shape[1] // rows):
            to_out[1, :, index * width : (index + 1) * width] = qo[
                0, index * rows : (index + 1) * rows, width:
            ]

    at_core(put, (kv, qo), (kv_beside, qo_beside))


def place_ffn_kernel(spots, up, down, up_beside, down_beside, to_up, to_down):
    def put(up, down):
        to_up[...] = up[0]
        to_down[...] = down[0]

    at_core(put, (up, down), (up_beside, down_beside))


def piece_specs(pieces):
    def spec(piece, core):
        return pl.BlockSpec((1,) + piece.shape[1:], lambda step, spots: (jnp.clip(step - core * 4, 0, 3), 0, 0))

    return [spec(piece, core) for core in range(2) for piece in pieces]


def row_spec(block, order, lead=0):
    if len(block) == 2:
        return pl.BlockSpec(block, lambda step, spots: (spots[order * 8 + step], 0))
    return pl.BlockSpec(block, lambda step, spots: (lead, spots[order * 8 + step], 0))


def place_call(kernel, memory, mine, beside, owns, own_specs, outs, out_specs):
    size = sum(math_prod(shape) for shape in outs)
    return pl.pallas_call(
        kernel,
        out_shape=[jax.ShapeDtypeStruct(shape, BF16) for shape in outs],
        grid_spec=pltpu.PrefetchScalarGridSpec(
            num_scalar_prefetch=1,
            grid=(8,),
            in_specs=piece_specs(mine) + own_specs,
            out_specs=out_specs,
        ),
        compiler_params=pltpu.CompilerParams(vmem_limit_bytes=memory << 20),
        cost_estimate=pl.CostEstimate(flops=0, bytes_accessed=size * 4, transcendentals=0),
    )(plane_places(False), *mine, *beside, *owns)


def math_prod(shape):
    total = 1
    for size in shape:
        total *= size
    return total


def fetch_attn(work, used, layer, w_query, w_key, w_value, w_out):
    count = plane_count()
    depth, width = w_query.shape[1], w_query.shape[2]
    rows, out_rows = depth // count, width // count
    parts = depth // width
    kv = jnp.concatenate([cut_piece(w_key, layer), cut_piece(w_value, layer)], 1)
    qo = jnp.concatenate([cut_piece(w_query, layer), cut_columns(cut_piece(w_out, layer), parts)], 1)
    token, span = yield
    moved = swap(after(jnp.concatenate([kv, qo], 1), token), "b")
    work.expect([moved], span)
    pieces = [moved[:, : 2 * width], moved[:, 2 * width :]]
    token = yield
    if small_plane() and out_rows % 16 == 0:
        mine, beside = yield from spread_steps(work, pieces, token)
        query, kv, out = place_call(
            place_attn_kernel,
            24 if layer else 56,
            mine,
            beside,
            (w_query, w_key, w_value, w_out),
            [row_spec((1, rows, width), order, layer) for order in (1, 0, 0)]
            + [row_spec((1, out_rows, depth), 1, layer)],
            ((depth, 2 * width), (depth, 4 * width), (2, width, depth)),
            [
                row_spec((rows, 2 * width), 1),
                row_spec((rows, 4 * width), 0),
                row_spec((2, out_rows, depth), 1),
            ],
        )
        used["attn", layer] = (query, kv, out.reshape(2 * width, depth))
        return
    packed = jnp.concatenate([lax.all_gather(piece, PLANE, axis=0) for piece in pieces], 2)
    kv, qo = packed[:, :, : 2 * width], packed[:, :, 2 * width :]
    out = qo[:, :, width:].reshape(count, parts, out_rows, width).transpose(0, 2, 1, 3).reshape(width, depth)
    kv = kv.reshape(depth, 2 * width)
    query = jnp.concatenate([w_query[layer], qo[:, :, :width].reshape(depth, width)], 1)
    kv = jnp.concatenate([w_key[layer], kv[:, :width], w_value[layer], kv[:, width:]], 1)
    used["attn", layer] = (query, kv, jnp.concatenate([w_out[layer], out], 0))


def fetch_ffn(work, used, layer, w_up, w_down):
    count = plane_count()
    depth, width = w_up.shape[1], w_up.shape[2]
    rows, down_rows = depth // count, width // count
    pieces = [cut_piece(weight, layer) for weight in (w_up, w_down)]
    for index, piece in enumerate(pieces):
        token, span = yield
        pieces[index] = swap(after(piece, token), "b")
        work.expect(pieces[index : index + 1], span)
    token = yield
    if small_plane() and width == depth:
        mine, beside = yield from spread_steps(work, pieces, token)
        used["ffn", layer] = place_call(
            place_ffn_kernel,
            24,
            mine,
            beside,
            (),
            [],
            ((depth, width), (width, depth)),
            [row_spec((rows, width), 0), row_spec((down_rows, depth), 1)],
        )
        return
    used["ffn", layer] = [lax.all_gather(piece, PLANE, axis=0, tiled=True) for piece in pieces]


def store_kernel(layout, arrays, given, spots, *refs):
    outs = refs[2 * arrays + given :]

    def put(*pieces):
        for out, (half, begin, width, turn) in zip(outs, layout):
            block = pieces[half][0, :, begin : begin + width].astype(F32)
            out[0] = block.T if turn else block

    at_core(put, refs[:arrays], refs[arrays : 2 * arrays])


def reduce_weights(work, results, name, layer, halves_of, layout):
    depth = halves_of[0][0][0].shape[1]
    widths = [[right.shape[1] // 2 for _, right in pairs] for pairs in halves_of]

    def side(value, half, which):
        parts, begin = [], 0
        for width in widths[half]:
            parts.append(value[:, begin + which * width : begin + (which + 1) * width])
            begin += 2 * width
        return jnp.concatenate(parts, 1)

    def grads_of(place, size, token):
        return [
            jnp.concatenate(
                [
                    dot_tn(lax.dynamic_slice_in_dim(left, place * size, size, 1), right)
                    for left, right in [(after(left, token), right) for left, right in pairs]
                ],
                1,
            ).astype(BF16)
            for pairs in halves_of
        ]

    token, span = yield
    if small_plane():
        core = lax.axis_index("c")
        size = depth // 2
        beside = [swap(grad, "c") for grad in grads_of(1 - core, size, token)]
        kept = grads_of(core, size, token)
        work.expect(kept + beside, span)

        def cut(half, other):
            index = lax.axis_index(ORDERS[half][0])
            begin = (1 - index if other else index) * (size // 2)
            return sum(
                lax.dynamic_slice_in_dim(value[half], begin, size // 2, 0).astype(F32) for value in (kept, beside)
            )

        token, span = yield
        kept, beside = after_all(kept, token), after_all(beside, token)
        got = [swap(cut(half, True).astype(BF16), ORDERS[half][0]) for half in range(2)]
        work.expect(got, span)
        near = [cut(half, False).astype(BF16) for half in range(2)]
        token, span = yield
        size = size // 4
        totals = [
            (value.astype(F32) + part.astype(F32)).astype(BF16)
            for value, part in zip(near, after_all(got, token))
        ]
        work.latest = totals[0]
        index = [lax.axis_index(order[1]) for order in ORDERS]
        got = [
            swap(lax.dynamic_slice_in_dim(value, (1 - i) * size, size, 0), order[1])
            for value, i, order in zip(totals, index, ORDERS)
        ]
        work.expect(got, span)
        near = [lax.dynamic_slice_in_dim(value, i * size, size, 0) for value, i in zip(totals, index)]
        token, span = yield
        totals = [
            (value.astype(F32) + part.astype(F32)).astype(BF16)
            for value, part in zip(near, after_all(got, token))
        ]
        work.latest = totals[0]
    else:
        totals = [
            lax.psum_scatter(grad, PLANE, scatter_dimension=0, tiled=True) for grad in grads_of(0, depth, token)
        ]
        token, span = yield
    other = jnp.concatenate([side(value, half, 1) for half, value in enumerate(totals)], 1)
    got = swap(after(other, token), "b")
    work.expect([got], span)
    token = yield
    other = after(got, token[0])
    pieces, begin = [], 0
    for half, value in enumerate(totals):
        own = side(value, half, 0)
        part = other[:, begin : begin + own.shape[1]]
        begin += own.shape[1]
        pieces.append((own.astype(F32) + part.astype(F32)).astype(BF16))
    work.latest = pieces[0]
    rows = depth // plane_count()
    shapes = [(LAYERS, w, depth) if turn else (LAYERS, depth, w) for _, _, w, turn in layout]
    if not (small_plane() and rows % 128 == 0):
        before = results.get(name)
        stored = []
        for index, (half, begin, width, turn) in enumerate(layout):
            block = lax.all_gather(pieces[half][:, begin : begin + width], PLANE, axis=0, tiled=True)
            block = block.astype(F32)
            block = block.T if turn else block
            base = jnp.zeros(shapes[index], F32) if before is None else before[index]
            stored.append(base.at[layer].set(block))
        results[name] = stored
        return
    mine, beside = yield from spread_steps(work, pieces, token)
    given = list(results.get(name) or [])
    size = sum(math_prod(shape) for shape in shapes) // LAYERS

    def out_spec(half, width, turn):
        if turn:
            return pl.BlockSpec((1, width, rows), lambda step, spots: (layer, 0, spots[half * 8 + step]))
        return row_spec((1, rows, width), half, layer)

    results[name] = pl.pallas_call(
        functools.partial(store_kernel, layout, len(mine), len(given)),
        out_shape=[jax.ShapeDtypeStruct(shape, F32) for shape in shapes],
        grid_spec=pltpu.PrefetchScalarGridSpec(
            num_scalar_prefetch=1,
            grid=(8,),
            in_specs=piece_specs(mine) + [pl.BlockSpec(memory_space=pl.ANY)] * len(given),
            out_specs=[out_spec(half, width, turn) for half, _, width, turn in layout],
        ),
        input_output_aliases={1 + len(mine + beside) + index: index for index in range(len(given))},
        compiler_params=pltpu.CompilerParams(vmem_limit_bytes=24 << 20),
        cost_estimate=pl.CostEstimate(flops=0, bytes_accessed=size * 6, transcendentals=0),
    )(plane_places(True), *mine, *beside, *given)
    work.expect(list(results[name]))


def halves(ref, size, columns, odd):
    count = ref.shape[0] // size
    return jnp.concatenate(
        [ref[index * size : (index + 1) * size, columns] for index in range(odd, count, 2)], 0
    )


def both_cores(mine, beside, size, columns, odd):
    return jnp.concatenate([halves(mine, size, columns, odd), halves(beside, size, columns, odd)], 0)


LOG2_E = 1.4426950408889634


def fill_bias(at_rows, at_keys, biases):
    for odd, bias in enumerate(biases):
        place, start = at_rows[:, 2 * odd : 2 * odd + 1], at_rows[:, 2 * odd + 1 : 2 * odd + 2]
        spots = at_keys[:, : bias.shape[1]]
        bias[...] = jnp.where((spots <= place) & (spots >= start), 0.0, -1e30)


def tile_scores(query, keys, bias, spots, slope):
    scores = lax.dot_general(query, keys, (((1,), (1,)), ((), ())), preferred_element_type=F32)
    return (scores * (HD ** (-0.5) * LOG2_E) + spots * (slope * LOG2_E)) + bias[...]


def attend_kernel(size, slopes, at_rows, at_keys, query, mine, beside, mixed, log_totals, *biases):
    fill_bias(at_rows, at_keys, biases)
    heads = query.shape[1] // HD
    for head in range(heads):
        columns = slice(head * HD, (head + 1) * HD)
        value_columns = slice((heads + head) * HD, (heads + head + 1) * HD)
        keys = [both_cores(mine, beside, size, columns, odd) for odd in range(2)]
        values = [both_cores(mine, beside, size, value_columns, odd) for odd in range(2)]
        for odd in range(2):
            key_rows = keys[0] if odd == 0 else jnp.concatenate(keys, 0)
            value_rows = values[0] if odd == 0 else jnp.concatenate(values, 0)
            spots = at_keys[:, : key_rows.shape[0]]
            scores = tile_scores(
                halves(query, size, columns, odd), key_rows, biases[odd], spots, slopes[head]
            )
            row_max = jnp.max(scores, axis=-1, keepdims=True)
            weights = jnp.exp2(scores - row_max)
            totals = jnp.sum(weights, axis=-1, keepdims=True)
            probabilities = (weights * (1.0 / totals)).astype(BF16)
            result = jnp.dot(probabilities, value_rows, preferred_element_type=F32).astype(BF16)
            logs = row_max + jnp.log2(totals)
            for index in range(result.shape[0] // size):
                rows = slice((2 * index + odd) * size, (2 * index + odd + 1) * size)
                mixed[rows, columns] = result[index * size : (index + 1) * size]
                log_totals[rows, head : head + 1] = logs[index * size : (index + 1) * size]


def attend_back_kernel(
    size, slopes, at_rows, at_keys, query, mine, beside, log_totals, grad, to_query, to_mine, to_beside, *biases
):
    fill_bias(at_rows, at_keys, biases)
    heads = query.shape[1] // HD
    scale = HD ** (-0.5)
    for head in range(heads):
        columns = slice(head * HD, (head + 1) * HD)
        value_columns = slice((heads + head) * HD, (heads + head + 1) * HD)
        one = slice(head, head + 1)
        keys = [both_cores(mine, beside, size, columns, odd) for odd in range(2)]
        values = [both_cores(mine, beside, size, value_columns, odd) for odd in range(2)]
        key_total = value_total = None
        for odd in (1, 0):
            key_rows = keys[0] if odd == 0 else jnp.concatenate(keys, 0)
            value_rows = values[0] if odd == 0 else jnp.concatenate(values, 0)
            query_rows = halves(query, size, columns, odd)
            grad_rows = halves(grad, size, columns, odd)
            scores = tile_scores(
                query_rows, key_rows, biases[odd], at_keys[:, : key_rows.shape[0]], slopes[head]
            )
            probabilities = jnp.exp2(scores - halves(log_totals, size, one, odd))
            grad_probs = lax.dot_general(
                grad_rows, value_rows, (((1,), (1,)), ((), ())), preferred_element_type=F32
            )
            centre = jnp.sum(grad_probs * probabilities, axis=-1, keepdims=True)
            grad_scores = (probabilities * (grad_probs - centre)).astype(BF16)
            grad_value = lax.dot_general(
                probabilities.astype(BF16), grad_rows, (((0,), (0,)), ((), ())), preferred_element_type=F32
            )
            grad_query = jnp.dot(grad_scores, key_rows, preferred_element_type=F32) * scale
            grad_key = (
                lax.dot_general(grad_scores, query_rows, (((0,), (0,)), ((), ())), preferred_element_type=F32)
                * scale
            )
            grad_query = grad_query.astype(BF16)
            for index in range(grad_query.shape[0] // size):
                rows = slice((2 * index + odd) * size, (2 * index + odd + 1) * size)
                to_query[rows, columns] = grad_query[index * size : (index + 1) * size]
            if odd == 1:
                early = keys[0].shape[0]
                results = [(grad_key[early:], grad_value[early:], 1)]
                key_total, value_total = grad_key[:early], grad_value[:early]
            else:
                results = [(grad_key + key_total, grad_value + value_total, 0)]
            for grad_key, grad_value, part in results:
                blocks = grad_key.shape[0] // size // 2
                for index in range(blocks):
                    rows = slice((2 * index + part) * size, (2 * index + part + 1) * size)
                    near = slice(index * size, (index + 1) * size)
                    far = slice((blocks + index) * size, (blocks + index + 1) * size)
                    to_mine[rows, columns] = grad_key[near]
                    to_mine[rows, value_columns] = grad_value[near]
                    to_beside[rows, columns] = grad_key[far].astype(BF16)
                    to_beside[rows, value_columns] = grad_value[far].astype(BF16)


def attention_cost(query, products):
    elements = query.shape[0] * query.shape[0] * 3 // 2 * (query.shape[1] // HD)
    return pl.CostEstimate(
        flops=elements * HD * 2 * products, bytes_accessed=query.size * 16, transcendentals=elements
    )


def bias_shapes(query, keys):
    return [pltpu.VMEM((query.shape[0] // 2, keys * (odd + 1) // 2), F32) for odd in range(2)]


def attention_specs(count):
    return [pl.BlockSpec(memory_space=pltpu.SMEM)] + [pl.BlockSpec(memory_space=pltpu.VMEM)] * count


def attend(query, mine, beside, info):
    slopes, at_rows, at_keys, size = info
    return pl.pallas_call(
        functools.partial(attend_kernel, size),
        out_shape=[
            jax.ShapeDtypeStruct(query.shape, BF16),
            jax.ShapeDtypeStruct((query.shape[0], query.shape[1] // HD), F32),
        ],
        in_specs=attention_specs(5),
        out_specs=[pl.BlockSpec(memory_space=pltpu.VMEM)] * 2,
        scratch_shapes=bias_shapes(query, at_keys.shape[1]),
        compiler_params=pltpu.CompilerParams(vmem_limit_bytes=48 << 20),
        cost_estimate=attention_cost(query, 2),
    )(slopes, at_rows, at_keys, query, mine, beside)


def attend_back(query, mine, beside, log_totals, grad_mixed, info):
    slopes, at_rows, at_keys, size = info
    return pl.pallas_call(
        functools.partial(attend_back_kernel, size),
        out_shape=[
            jax.ShapeDtypeStruct(query.shape, BF16),
            jax.ShapeDtypeStruct(mine.shape, F32),
            jax.ShapeDtypeStruct(mine.shape, BF16),
        ],
        in_specs=attention_specs(7),
        out_specs=[pl.BlockSpec(memory_space=pltpu.VMEM)] * 3,
        scratch_shapes=bias_shapes(query, at_keys.shape[1]),
        compiler_params=pltpu.CompilerParams(vmem_limit_bytes=48 << 20),
        cost_estimate=attention_cost(query, 5),
    )(slopes, at_rows, at_keys, query, mine, beside, log_totals, grad_mixed)


def attention_info(lengths, slopes, size):
    block, core = lax.axis_index("b"), lax.axis_index("c")
    ends = jnp.cumsum(jnp.where(core == block, lengths, swap(lengths, "c")))
    across = lax.axis_size("r")
    steps = jnp.arange(size, dtype=jnp.int32)

    def spots(which, odd):
        return jnp.concatenate([((odd * across + place) * 2 + which) * size + steps for place in axis_order("r")])

    columns, keys = [], []
    for odd in range(2):
        place = spots(core, odd)
        start = jnp.max(jnp.where(place[:, None] >= ends[None, :], ends[None, :], 0), axis=1)
        columns += [place, start]
        keys += [spots(which, odd) for which in axis_order("c")]
    at_rows = jnp.stack(columns, 1).astype(F32)
    at_keys = jnp.concatenate(keys)[None, :].astype(F32)
    return slopes, at_rows, at_keys, size


def local(
    activations,
    lengths,
    cotangent,
    gain_attn,
    shift_attn,
    w_query,
    b_query,
    w_key,
    w_value,
    b_value,
    w_out,
    b_out,
    gain_ffn,
    shift_ffn,
    w_up,
    b_up,
    w_down,
    b_down,
):
    block, place = lax.axis_index("b"), lax.axis_index("r")
    across = lax.axis_size("r")
    shards = [block * across + place, (1 - block) * across + place]
    head_width = w_query.shape[2]
    head_count = head_width // HD
    hidden_width = w_up.shape[2]

    head_ids = jnp.concatenate(
        [shard * head_count + jnp.arange(head_count, dtype=jnp.int32) for shard in shards]
    ).astype(F32)
    slopes = 2.0 ** (-8.0 * (head_ids + 1.0) / H)
    info = attention_info(lengths[0], slopes, activations.shape[0] // 2)

    bias_own = jnp.concatenate([b_query, b_value], 1)
    bias_other = swap(bias_own, "b")

    used, results = {}, {}
    work = Background()
    for layer in range(LAYERS):
        work.add(
            fetch_attn(work, used, layer, w_query, w_key, w_value, w_out),
            FETCH_ATTN[layer],
        )
        work.add(fetch_ffn(work, used, layer, w_up, w_down), FETCH_FFN[layer])

    def move(name, steps, value):
        token, span = yield
        steps = steps(value, token)
        work.expect(next(steps), span)
        results[name] = next(steps)

    moving = to_chunks(activations, None, lambda value: work.at("r", value))
    next(moving)
    stream = work.at("s", next(moving).astype(F32))
    work.add(move("cotangent", to_chunks, cotangent), (COTANGENT,))

    def rows_of(array, first, last):
        size = array.shape[0] // across
        return array[first * size : last * size]

    stored = []
    zero = jnp.zeros((2 * head_width,), F32)
    for layer in range(LAYERS):
        bias_query = jnp.concatenate([bias_own[layer, :head_width], bias_other[layer, :head_width]])
        bias_kv = jnp.concatenate([zero, bias_own[layer, head_width:], bias_other[layer, head_width:]])
        bias_up = [
            lax.dynamic_slice_in_dim(b_up[layer], shard * hidden_width, hidden_width, 0) for shard in shards
        ]
        unit, inverse = norm_parts(stream)
        inputs = gather_rows((unit * gain_attn[layer] + shift_attn[layer]).astype(BF16), work, str(layer) + "a")
        weight_query, weight_kv, weight_out = used["attn", layer]
        mine = (dot(inputs, weight_kv) + bias_kv).astype(BF16)
        mine = work.at(str(layer) + "b", mine)
        beside = swap(mine, "c")
        query = (dot(inputs, weight_query) + bias_query).astype(BF16)
        mixed, log_totals = attend(query, mine, beside, info)
        middle = stream + (
            scatter_rows(lambda first, last: dot(rows_of(mixed, first, last), weight_out), work, str(layer) + "c") + b_out[layer]
        )
        unit_mid, inverse_mid = norm_parts(middle)
        inputs_mid = gather_rows((unit_mid * gain_ffn[layer] + shift_ffn[layer]).astype(BF16), work, str(layer) + "d")
        ups, downs = zip((w_up[layer], w_down[layer]), used["ffn", layer])
        hidden = [dot(inputs_mid, up) + bias for up, bias in zip(ups, bias_up)]
        active = [gelu_tanh(value).astype(BF16) for value in hidden]
        hidden = [value.astype(BF16) for value in hidden]
        stream = middle + (
            scatter_rows(lambda first, last: sum(dot(rows_of(value, first, last), down) for value, down in zip(active, downs)),
                work, str(layer) + "e") + b_down[layer]
        )
        stored.append(
            (
                unit,
                inverse,
                inputs,
                query,
                mine,
                beside,
                mixed,
                log_totals,
                unit_mid,
                inverse_mid,
                inputs_mid,
                hidden,
                active,
            )
        )
    work.add(move("activations_out", from_chunks, stream.astype(BF16)), (ACTIVATIONS_OUT,))
    grad_stream = results["cotangent"].astype(F32)
    small = {}
    for layer in reversed(range(LAYERS)):
        weight_query, weight_kv, weight_out = used["attn", layer]
        ups, downs = zip((w_up[layer], w_down[layer]), used["ffn", layer])
        (
            unit,
            inverse,
            inputs,
            query,
            mine,
            beside,
            mixed,
            log_totals,
            unit_mid,
            inverse_mid,
            inputs_mid,
            hidden,
            active,
        ) = stored[layer]
        grad_branch = grad_stream.astype(BF16)
        grad_b_down = jnp.sum(grad_branch, axis=0, dtype=F32)
        branch_all = gather_rows(grad_branch, work, str(layer) + "f")
        grad_hidden = [
            jax.vjp(gelu_tanh, value.astype(F32))[1](dot_nt(branch_all, down))[0].astype(BF16)
            for value, down in zip(hidden, downs)
        ]
        work.add(
            reduce_weights(
                work,
                results,
                "ffn",
                layer,
                ([(inputs_mid, jnp.concatenate(grad_hidden, 1))], [(branch_all, jnp.concatenate(active, 1))]),
                ((0, 0, hidden_width, False), (1, 0, hidden_width, True)),
            ),
            REDUCE_FFN[layer],
        )
        grad_normed_mid = scatter_rows(
            lambda first, last: sum(dot_nt(rows_of(value, first, last), up) for value, up in zip(grad_hidden, ups)),
            work,
            str(layer) + "g",
        )
        grad_b_up = jnp.concatenate([jnp.sum(value, axis=0, dtype=F32) for value in grad_hidden])
        grad_gain_ffn = jnp.sum(grad_normed_mid * unit_mid, axis=0)
        grad_shift_ffn = jnp.sum(grad_normed_mid, axis=0)
        grad_middle = grad_stream + norm_back(grad_normed_mid, unit_mid, inverse_mid, gain_ffn[layer])
        grad_attn = grad_middle.astype(BF16)
        grad_b_out = jnp.sum(grad_attn, axis=0, dtype=F32)
        attn_all = gather_rows(grad_attn, work, str(layer) + "h")
        grad_mixed = dot_nt(attn_all, weight_out).astype(BF16)
        grad_query, grad_mine, grad_beside = attend_back(query, mine, beside, log_totals, grad_mixed, info)
        grad_beside = work.at(str(layer) + "i", grad_beside)
        grad_kv = (grad_mine + swap(grad_beside, "c").astype(F32)).astype(BF16)
        work.add(
            reduce_weights(
                work,
                results,
                "attn",
                layer,
                (
                    [(inputs, grad_kv[:, : 2 * head_width]), (inputs, grad_kv[:, 2 * head_width :])],
                    [(inputs, grad_query), (attn_all, mixed)],
                ),
                (
                    (1, 0, head_width, False),
                    (0, 0, head_width, False),
                    (0, head_width, head_width, False),
                    (1, head_width, head_width, True),
                ),
            ),
            REDUCE_ATTN[layer],
        )
        grad_normed = scatter_rows(
            lambda first, last: dot_nt(rows_of(grad_query, first, last), weight_query)
            + dot_nt(rows_of(grad_kv, first, last), weight_kv),
            work,
            str(layer) + "j",
        )
        grad_b_query = jnp.sum(grad_query, axis=0, dtype=F32)
        grad_b_value = jnp.sum(grad_kv[:, 2 * head_width :], axis=0, dtype=F32)
        grads_in = grad_normed
        grad_gain_attn = jnp.sum(grad_normed * unit, axis=0)
        grad_shift_attn = jnp.sum(grad_normed, axis=0)
        grad_stream = grad_middle + norm_back(grad_normed, unit, inverse, gain_attn[layer])

        def spread(values, total):
            width = values.shape[0] // 2
            result = jnp.zeros((total,), F32)
            for index, shard in enumerate(shards):
                result = lax.dynamic_update_slice_in_dim(
                    result, values[index * width : (index + 1) * width], shard * width, 0
                )
            return result

        whole = head_width * 2 * across
        packed = jnp.concatenate(
            [
                grad_gain_attn,
                grad_shift_attn,
                grad_b_out,
                grad_gain_ffn,
                grad_shift_ffn,
                grad_b_down,
                spread(grad_b_query, whole),
                spread(grad_b_value, whole),
                spread(grad_b_up, b_up.shape[1]),
            ]
        )
        small[layer] = packed.reshape(-1, 128)

    work.add(sum_small(work, results, jnp.stack([small[layer] for layer in range(LAYERS)])), SUM_SMALL)
    work.at("t1", grads_in)
    leaving = from_chunks(grad_stream.astype(BF16), None)
    next(leaving)
    input_grad = next(leaving)
    for step in range(2, 7):
        work.at("t" + str(step), work.latest)
    assert not work.tasks
    attn_outs, ffn_outs = results["attn"], results["ffn"]
    table = results["small"].reshape(LAYERS, -1)
    wide = gain_attn.shape[1]
    shared = [table[:, index * wide : (index + 1) * wide] for index in range(6)]
    begin = 6 * wide
    whole = head_width * 2 * across
    home = shards[0]
    all_b_query = lax.dynamic_slice_in_dim(table[:, begin : begin + whole], home * head_width, head_width, 1)
    begin += whole
    all_b_value = lax.dynamic_slice_in_dim(table[:, begin : begin + whole], home * head_width, head_width, 1)
    begin += whole
    all_b_up = lax.dynamic_slice_in_dim(table[:, begin:], home * hidden_width, hidden_width, 1)
    return (
        results["activations_out"],
        input_grad,
        shared[0],
        shared[1],
        attn_outs[0],
        all_b_query,
        attn_outs[1],
        attn_outs[2],
        all_b_value,
        attn_outs[3],
        shared[2],
        shared[3],
        shared[4],
        ffn_outs[0],
        all_b_up,
        ffn_outs[1],
        shared[5],
    )


def solution(mesh):
    groups, parts = mesh.shape["dp"], mesh.shape["mp"]
    fine = Mesh(
        mesh.devices.reshape(2, groups // 4, 2, 2, parts // 2), ("ky", "kx", "c", "b", "r")
    )
    dp, mp = ("ky", "kx", "c"), ("b", "r")
    rows, whole = P(dp + mp, None), P()
    columns3, columns2, rows3 = P(None, None, mp), P(None, mp), P(None, mp, None)
    return jax.shard_map(
        local,
        mesh=fine,
        in_specs=(
            rows,
            P(dp, None),
            rows,
            whole,
            whole,
            columns3,
            columns2,
            columns3,
            columns3,
            columns2,
            rows3,
            whole,
            whole,
            whole,
            columns3,
            whole,
            rows3,
            whole,
        ),
        out_specs=(
            rows,
            rows,
            whole,
            whole,
            columns3,
            columns2,
            columns3,
            columns3,
            columns2,
            rows3,
            whole,
            whole,
            whole,
            columns3,
            columns2,
            rows3,
            whole,
        ),
        check_vma=False,
    )
```

```python
import functools

import jax
import jax.numpy as jnp
from jax import lax
from jax.experimental import pallas as pl
from jax.experimental.pallas import tpu as pltpu
from jax.sharding import Mesh
from jax.sharding import PartitionSpec as P

H = 8
HD = 128
LAYERS = 2
norm_eps = 1e-05
F32 = jnp.float32
BF16 = jnp.bfloat16
PLANE = ("c", "kx", "ky")
FETCH_ATTN = ("r", "0a", None, None), ("0c", "0d", "0e", "1a")
FETCH_FFN = (("s", 3), "0b", "0c", "0d", "0d2"), ("0e", (None, 1), "1a", "1c", "1c2")
COTANGENT = "1c"
ACTIVATIONS_OUT = "1f"
REDUCE_FFN = (
    ("0g", ("0h", 3), ("0j", 2), ("t1", 2), "t2", "t3", "t5"),
    ("1g", ("1h", 2), ("1i", 2), ("0f", 3), "0g", ("0g2", 2), "0j"),
)
REDUCE_ATTN = (
    ("0j", ("0j2", 2), "t2", "t3", "t4", "t5", "t6"),
    ("1j", "0f", ("0f2", 2), "0g", ("0h2", 2), ("0j2", 2), "t3"),
)
SUM_SMALL = ("t1", "t2", "t3", "t4", "t5", "t6")


def gelu_tanh(values):
    return jax.nn.gelu(values, approximate=True)


def norm_parts(stream):
    centred = stream - jnp.mean(stream, axis=-1, keepdims=True)
    inverse = lax.rsqrt(jnp.mean(centred * centred, axis=-1, keepdims=True) + norm_eps)
    return centred * inverse, inverse


def norm_back(grad_normed, unit_rows, inverse, gain):
    scaled = grad_normed * gain
    return inverse * (
        scaled
        - jnp.mean(scaled, axis=-1, keepdims=True)
        - unit_rows * jnp.mean(scaled * unit_rows, axis=-1, keepdims=True)
    )


def dot(left, right):
    return jnp.dot(left, right, preferred_element_type=F32)


def dot_nt(left, right):
    return jnp.einsum("ti,oi->to", left, right, preferred_element_type=F32)


def dot_tn(left, right):
    return jnp.einsum("ti,to->io", left, right, preferred_element_type=F32)


def after(value, other):
    return value if other is None else lax.optimization_barrier((value, other))[0]


def swap(value, axis):
    return lax.ppermute(value, axis, [(0, 1), (1, 0)])


def small_plane():
    return all(lax.axis_size(axis) == 2 for axis in PLANE)


def axis_order(axis):
    size = lax.axis_size(axis)
    if size == 2:
        return [lax.axis_index(axis), 1 - lax.axis_index(axis)]
    return list(range(size))


def gather_rows(rows, work, event):
    rows = work.at(event, rows)
    if lax.axis_size("r") == 2:
        across = work.at(event + "2", swap(rows, "r"))
        return jnp.concatenate([rows, across], 0)
    return work.at(event + "2", lax.all_gather(rows, "r", axis=0, tiled=True))


def scatter_rows(product, work, event):
    count = lax.axis_size("r")
    if count == 2:
        send = work.at(event, product(1, 2).astype(BF16))
        across = swap(send, "r")
        near = product(0, 1)
        return near + work.at(event + "2", across).astype(F32)
    partial = work.at(event, product(0, count).astype(BF16))
    across = lax.psum_scatter(partial, "r", scatter_dimension=0, tiled=True)
    return work.at(event + "2", across).astype(F32)


def to_chunks(value, token, at=lambda value: value):
    half = value.shape[0] // 2
    value = after(value, token)
    low, high = value[:half], value[half:]
    core, block = lax.axis_index("c"), lax.axis_index("b")
    first = jnp.where(block == 0, low, high)
    second = jnp.where(block == 0, high, low)
    first = at(first)
    first = lax.ppermute(first, ("c", "b"), [(0, 0), (1, 2), (2, 1), (3, 3)])
    second = lax.ppermute(second, ("c", "b"), [(0, 2), (1, 0), (2, 3), (3, 1)])
    yield [first, second]
    yield jnp.where(core == 0, jnp.concatenate([first, second], 0), jnp.concatenate([second, first], 0))


def from_chunks(rows, token):
    half = rows.shape[0] // 2
    rows = after(rows, token)
    early, late = rows[:half], rows[half:]
    core, block = lax.axis_index("c"), lax.axis_index("b")
    first = jnp.where(core == 0, early, late)
    second = jnp.where(core == 0, late, early)
    first = lax.ppermute(first, ("c", "b"), [(0, 0), (2, 1), (1, 2), (3, 3)])
    second = lax.ppermute(second, ("c", "b"), [(2, 0), (0, 1), (3, 2), (1, 3)])
    yield [first, second]
    yield jnp.where(block == 0, jnp.concatenate([first, second], 0), jnp.concatenate([second, first], 0))


def plane_count():
    return lax.axis_size("c") * lax.axis_size("kx") * lax.axis_size("ky")


def plane_place(c=None, x=None, y=None):
    c = lax.axis_index("c") if c is None else c
    x = lax.axis_index("kx") if x is None else x
    y = lax.axis_index("ky") if y is None else y
    return (c * lax.axis_size("kx") + x) * lax.axis_size("ky") + y


ORDERS = (("kx", "ky"), ("ky", "kx"))


def plane_places(ordered):
    spots = []
    for first, second in ORDERS:
        for c in axis_order("c"):
            for slow in axis_order(second):
                for fast in axis_order(first):
                    if ordered:
                        spots.append((c * 2 + fast) * 2 + slow)
                    else:
                        spots.append(plane_place(c, **{first[1]: fast, second[1]: slow}))
    return jnp.stack(spots).astype(jnp.int32)


def after_all(values, token):
    return [after(value, token) for value in values]


def spread_steps(work, pieces, token):
    token, span = token
    pieces = [piece[None] for piece in pieces]
    for stage in range(2):
        pieces = after_all(pieces, token)
        got = [swap(piece, order[stage]) for piece, order in zip(pieces, ORDERS)]
        work.expect(got, span)
        token, span = yield
        got = after_all(got, token)
        pieces = [jnp.concatenate(pair, 0) for pair in zip(pieces, got)]
        work.latest = pieces[0]
    return pieces, [swap(piece, "c") for piece in pieces]


class Background:
    def __init__(self):
        self.tasks = []
        self.waiting = []
        self.step = 0

    def advance(self, task, events, token):
        try:
            task.send(token)
            while events and (events[0] is None or events[0][0] is None):
                event = events.pop(0)
                task.send((None, event[1] if event else 1))
            self.tasks.append((task, events))
        except StopIteration:
            pass

    def add(self, task, events):
        self.advance(task, list(events), None)

    def expect(self, values, span=1):
        self.waiting += [(self.step + span, value) for value in values]

    def at(self, event, value):
        self.step += 1
        for due, result in self.waiting:
            if due <= self.step:
                value = after(value, result)
        self.waiting = [pair for pair in self.waiting if pair[0] > self.step]
        tasks, self.tasks = self.tasks, []
        for task, events in tasks:
            name, span = (events[0], 1) if isinstance(events[0], str) else events[0]
            if name == event:
                self.advance(task, events[1:], (value, span))
            else:
                self.tasks.append((task, events))
        return value


def sum_small(work, results, value):
    for axis in ("c", "kx", "ky", "r", "b"):
        token, span = yield
        value = after(value, token)
        if lax.axis_size(axis) == 2:
            got = swap(value, axis)
            work.expect([got], span)
            value = value + got
        else:
            value = lax.psum(value, axis)
    token, span = yield
    results["small"] = value


def cut_columns(value, parts):
    width = value.shape[1] // parts
    return jnp.concatenate([value[:, index * width : (index + 1) * width] for index in range(parts)], 0)


def cut_piece(weight, layer):
    size = weight.shape[1] // plane_count()
    return lax.dynamic_slice(weight, (layer, plane_place() * size, 0), (1, size, weight.shape[2]))[0]


def at_core(put, mine, beside):
    @pl.when(pl.program_id(0) < 4)
    def _():
        put(*mine)

    @pl.when(pl.program_id(0) >= 4)
    def _():
        put(*beside)


def place_attn_kernel(spots, kv, qo, kv_beside, qo_beside, query, key, value, out, to_query, to_kv, to_out):
    width = query.shape[2]
    rows = out.shape[1]

    def put(kv, qo):
        to_kv[:, :width] = key[0]
        to_kv[:, width : 2 * width] = kv[0, :, :width]
        to_kv[:, 2 * width : 3 * width] = value[0]
        to_kv[:, 3 * width :] = kv[0, :, width:]
        to_query[:, :width] = query[0]
        to_query[:, width:] = qo[0, :, :width]
        to_out[0] = out[0]
        for index in range(qo.shape[1] // rows):
            to_out[1, :, index * width : (index + 1) * width] = qo[
                0, index * rows : (index + 1) * rows, width:
            ]

    at_core(put, (kv, qo), (kv_beside, qo_beside))


def place_ffn_kernel(spots, up, down, up_beside, down_beside, to_up, to_down):
    def put(up, down):
        to_up[...] = up[0]
        to_down[...] = down[0]

    at_core(put, (up, down), (up_beside, down_beside))


def piece_specs(pieces):
    def spec(piece, core):
        return pl.BlockSpec((1,) + piece.shape[1:], lambda step, spots: (jnp.clip(step - core * 4, 0, 3), 0, 0))

    return [spec(piece, core) for core in range(2) for piece in pieces]


def row_spec(block, order, lead=0):
    if len(block) == 2:
        return pl.BlockSpec(block, lambda step, spots: (spots[order * 8 + step], 0))
    return pl.BlockSpec(block, lambda step, spots: (lead, spots[order * 8 + step], 0))


def place_call(kernel, memory, mine, beside, owns, own_specs, outs, out_specs):
    size = sum(math_prod(shape) for shape in outs)
    return pl.pallas_call(
        kernel,
        out_shape=[jax.ShapeDtypeStruct(shape, BF16) for shape in outs],
        grid_spec=pltpu.PrefetchScalarGridSpec(
            num_scalar_prefetch=1,
            grid=(8,),
            in_specs=piece_specs(mine) + own_specs,
            out_specs=out_specs,
        ),
        compiler_params=pltpu.CompilerParams(vmem_limit_bytes=memory << 20),
        cost_estimate=pl.CostEstimate(flops=0, bytes_accessed=size * 4, transcendentals=0),
    )(plane_places(False), *mine, *beside, *owns)


def math_prod(shape):
    total = 1
    for size in shape:
        total *= size
    return total


def fetch_attn(work, used, layer, w_query, w_key, w_value, w_out):
    count = plane_count()
    depth, width = w_query.shape[1], w_query.shape[2]
    rows, out_rows = depth // count, width // count
    parts = depth // width
    kv = jnp.concatenate([cut_piece(w_key, layer), cut_piece(w_value, layer)], 1)
    qo = jnp.concatenate([cut_piece(w_query, layer), cut_columns(cut_piece(w_out, layer), parts)], 1)
    token, span = yield
    moved = swap(after(jnp.concatenate([kv, qo], 1), token), "b")
    work.expect([moved], span)
    pieces = [moved[:, : 2 * width], moved[:, 2 * width :]]
    token = yield
    if small_plane() and out_rows % 16 == 0:
        mine, beside = yield from spread_steps(work, pieces, token)
        query, kv, out = place_call(
            place_attn_kernel,
            24 if layer else 56,
            mine,
            beside,
            (w_query, w_key, w_value, w_out),
            [row_spec((1, rows, width), order, layer) for order in (1, 0, 0)]
            + [row_spec((1, out_rows, depth), 1, layer)],
            ((depth, 2 * width), (depth, 4 * width), (2, width, depth)),
            [
                row_spec((rows, 2 * width), 1),
                row_spec((rows, 4 * width), 0),
                row_spec((2, out_rows, depth), 1),
            ],
        )
        used["attn", layer] = (query, kv, out.reshape(2 * width, depth))
        return
    packed = jnp.concatenate([lax.all_gather(piece, PLANE, axis=0) for piece in pieces], 2)
    kv, qo = packed[:, :, : 2 * width], packed[:, :, 2 * width :]
    out = qo[:, :, width:].reshape(count, parts, out_rows, width).transpose(0, 2, 1, 3).reshape(width, depth)
    kv = kv.reshape(depth, 2 * width)
    query = jnp.concatenate([w_query[layer], qo[:, :, :width].reshape(depth, width)], 1)
    kv = jnp.concatenate([w_key[layer], kv[:, :width], w_value[layer], kv[:, width:]], 1)
    used["attn", layer] = (query, kv, jnp.concatenate([w_out[layer], out], 0))


def fetch_ffn(work, used, layer, w_up, w_down):
    count = plane_count()
    depth, width = w_up.shape[1], w_up.shape[2]
    rows, down_rows = depth // count, width // count
    pieces = [cut_piece(weight, layer) for weight in (w_up, w_down)]
    for index, piece in enumerate(pieces):
        token, span = yield
        pieces[index] = swap(after(piece, token), "b")
        work.expect(pieces[index : index + 1], span)
    token = yield
    if small_plane() and width == depth:
        mine, beside = yield from spread_steps(work, pieces, token)
        used["ffn", layer] = place_call(
            place_ffn_kernel,
            24,
            mine,
            beside,
            (),
            [],
            ((depth, width), (width, depth)),
            [row_spec((rows, width), 0), row_spec((down_rows, depth), 1)],
        )
        return
    used["ffn", layer] = [lax.all_gather(piece, PLANE, axis=0, tiled=True) for piece in pieces]


def store_kernel(layout, arrays, given, spots, *refs):
    outs = refs[2 * arrays + given :]

    def put(*pieces):
        for out, (half, begin, width, turn) in zip(outs, layout):
            block = pieces[half][0, :, begin : begin + width].astype(F32)
            out[0] = block.T if turn else block

    at_core(put, refs[:arrays], refs[arrays : 2 * arrays])


def reduce_weights(work, results, name, layer, halves_of, layout):
    depth = halves_of[0][0][0].shape[1]
    widths = [[right.shape[1] // 2 for _, right in pairs] for pairs in halves_of]

    def side(value, half, which):
        parts, begin = [], 0
        for width in widths[half]:
            parts.append(value[:, begin + which * width : begin + (which + 1) * width])
            begin += 2 * width
        return jnp.concatenate(parts, 1)

    def grads_of(place, size, token):
        return [
            jnp.concatenate(
                [
                    dot_tn(lax.dynamic_slice_in_dim(left, place * size, size, 1), right)
                    for left, right in [(after(left, token), right) for left, right in pairs]
                ],
                1,
            ).astype(BF16)
            for pairs in halves_of
        ]

    token, span = yield
    if small_plane():
        core = lax.axis_index("c")
        size = depth // 2
        beside = [swap(grad, "c") for grad in grads_of(1 - core, size, token)]
        kept = grads_of(core, size, token)
        work.expect(kept + beside, span)

        def cut(half, other):
            index = lax.axis_index(ORDERS[half][0])
            begin = (1 - index if other else index) * (size // 2)
            return sum(
                lax.dynamic_slice_in_dim(value[half], begin, size // 2, 0).astype(F32) for value in (kept, beside)
            )

        token, span = yield
        kept, beside = after_all(kept, token), after_all(beside, token)
        got = [swap(cut(half, True).astype(BF16), ORDERS[half][0]) for half in range(2)]
        work.expect(got, span)
        near = [cut(half, False).astype(BF16) for half in range(2)]
        token, span = yield
        size = size // 4
        totals = [
            (value.astype(F32) + part.astype(F32)).astype(BF16)
            for value, part in zip(near, after_all(got, token))
        ]
        work.latest = totals[0]
        index = [lax.axis_index(order[1]) for order in ORDERS]
        got = [
            swap(lax.dynamic_slice_in_dim(value, (1 - i) * size, size, 0), order[1])
            for value, i, order in zip(totals, index, ORDERS)
        ]
        work.expect(got, span)
        near = [lax.dynamic_slice_in_dim(value, i * size, size, 0) for value, i in zip(totals, index)]
        token, span = yield
        totals = [
            (value.astype(F32) + part.astype(F32)).astype(BF16)
            for value, part in zip(near, after_all(got, token))
        ]
        work.latest = totals[0]
    else:
        totals = [
            lax.psum_scatter(grad, PLANE, scatter_dimension=0, tiled=True) for grad in grads_of(0, depth, token)
        ]
        token, span = yield
    other = jnp.concatenate([side(value, half, 1) for half, value in enumerate(totals)], 1)
    got = swap(after(other, token), "b")
    work.expect([got], span)
    token = yield
    other = after(got, token[0])
    pieces, begin = [], 0
    for half, value in enumerate(totals):
        own = side(value, half, 0)
        part = other[:, begin : begin + own.shape[1]]
        begin += own.shape[1]
        pieces.append((own.astype(F32) + part.astype(F32)).astype(BF16))
    work.latest = pieces[0]
    rows = depth // plane_count()
    shapes = [(LAYERS, w, depth) if turn else (LAYERS, depth, w) for _, _, w, turn in layout]
    if not (small_plane() and rows % 128 == 0):
        before = results.get(name)
        stored = []
        for index, (half, begin, width, turn) in enumerate(layout):
            block = lax.all_gather(pieces[half][:, begin : begin + width], PLANE, axis=0, tiled=True)
            block = block.astype(F32)
            block = block.T if turn else block
            base = jnp.zeros(shapes[index], F32) if before is None else before[index]
            stored.append(base.at[layer].set(block))
        results[name] = stored
        return
    mine, beside = yield from spread_steps(work, pieces, token)
    given = list(results.get(name) or [])
    size = sum(math_prod(shape) for shape in shapes) // LAYERS

    def out_spec(half, width, turn):
        if turn:
            return pl.BlockSpec((1, width, rows), lambda step, spots: (layer, 0, spots[half * 8 + step]))
        return row_spec((1, rows, width), half, layer)

    results[name] = pl.pallas_call(
        functools.partial(store_kernel, layout, len(mine), len(given)),
        out_shape=[jax.ShapeDtypeStruct(shape, F32) for shape in shapes],
        grid_spec=pltpu.PrefetchScalarGridSpec(
            num_scalar_prefetch=1,
            grid=(8,),
            in_specs=piece_specs(mine) + [pl.BlockSpec(memory_space=pl.ANY)] * len(given),
            out_specs=[out_spec(half, width, turn) for half, _, width, turn in layout],
        ),
        input_output_aliases={1 + len(mine + beside) + index: index for index in range(len(given))},
        compiler_params=pltpu.CompilerParams(vmem_limit_bytes=24 << 20),
        cost_estimate=pl.CostEstimate(flops=0, bytes_accessed=size * 6, transcendentals=0),
    )(plane_places(True), *mine, *beside, *given)
    work.expect(list(results[name]))


def halves(ref, size, columns, odd):
    count = ref.shape[0] // size
    return jnp.concatenate(
        [ref[index * size : (index + 1) * size, columns] for index in range(odd, count, 2)], 0
    )


def both_cores(mine, beside, size, columns, odd):
    return jnp.concatenate([halves(mine, size, columns, odd), halves(beside, size, columns, odd)], 0)


LOG2_E = 1.4426950408889634


def fill_bias(at_rows, at_keys, biases):
    for odd, bias in enumerate(biases):
        place, start = at_rows[:, 2 * odd : 2 * odd + 1], at_rows[:, 2 * odd + 1 : 2 * odd + 2]
        spots = at_keys[:, : bias.shape[1]]
        bias[...] = jnp.where((spots <= place) & (spots >= start), 0.0, -1e30)


def tile_scores(query, keys, bias, spots, slope):
    scores = lax.dot_general(query, keys, (((1,), (1,)), ((), ())), preferred_element_type=F32)
    return (scores * (HD ** (-0.5) * LOG2_E) + spots * (slope * LOG2_E)) + bias[...]


def attend_kernel(size, slopes, at_rows, at_keys, query, mine, beside, mixed, log_totals, *biases):
    fill_bias(at_rows, at_keys, biases)
    heads = query.shape[1] // HD
    for head in range(heads):
        columns = slice(head * HD, (head + 1) * HD)
        value_columns = slice((heads + head) * HD, (heads + head + 1) * HD)
        keys = [both_cores(mine, beside, size, columns, odd) for odd in range(2)]
        values = [both_cores(mine, beside, size, value_columns, odd) for odd in range(2)]
        for odd in range(2):
            key_rows = keys[0] if odd == 0 else jnp.concatenate(keys, 0)
            value_rows = values[0] if odd == 0 else jnp.concatenate(values, 0)
            spots = at_keys[:, : key_rows.shape[0]]
            scores = tile_scores(
                halves(query, size, columns, odd), key_rows, biases[odd], spots, slopes[head]
            )
            row_max = jnp.max(scores, axis=-1, keepdims=True)
            weights = jnp.exp2(scores - row_max)
            totals = jnp.sum(weights, axis=-1, keepdims=True)
            probabilities = (weights * (1.0 / totals)).astype(BF16)
            result = jnp.dot(probabilities, value_rows, preferred_element_type=F32).astype(BF16)
            logs = row_max + jnp.log2(totals)
            for index in range(result.shape[0] // size):
                rows = slice((2 * index + odd) * size, (2 * index + odd + 1) * size)
                mixed[rows, columns] = result[index * size : (index + 1) * size]
                log_totals[rows, head : head + 1] = logs[index * size : (index + 1) * size]


def attend_back_kernel(
    size, slopes, at_rows, at_keys, query, mine, beside, log_totals, grad, to_query, to_mine, to_beside, *biases
):
    fill_bias(at_rows, at_keys, biases)
    heads = query.shape[1] // HD
    scale = HD ** (-0.5)
    for head in range(heads):
        columns = slice(head * HD, (head + 1) * HD)
        value_columns = slice((heads + head) * HD, (heads + head + 1) * HD)
        one = slice(head, head + 1)
        keys = [both_cores(mine, beside, size, columns, odd) for odd in range(2)]
        values = [both_cores(mine, beside, size, value_columns, odd) for odd in range(2)]
        key_total = value_total = None
        for odd in (1, 0):
            key_rows = keys[0] if odd == 0 else jnp.concatenate(keys, 0)
            value_rows = values[0] if odd == 0 else jnp.concatenate(values, 0)
            query_rows = halves(query, size, columns, odd)
            grad_rows = halves(grad, size, columns, odd)
            scores = tile_scores(
                query_rows, key_rows, biases[odd], at_keys[:, : key_rows.shape[0]], slopes[head]
            )
            probabilities = jnp.exp2(scores - halves(log_totals, size, one, odd))
            grad_probs = lax.dot_general(
                grad_rows, value_rows, (((1,), (1,)), ((), ())), preferred_element_type=F32
            )
            centre = jnp.sum(grad_probs * probabilities, axis=-1, keepdims=True)
            grad_scores = (probabilities * (grad_probs - centre)).astype(BF16)
            grad_value = lax.dot_general(
                probabilities.astype(BF16), grad_rows, (((0,), (0,)), ((), ())), preferred_element_type=F32
            )
            grad_query = jnp.dot(grad_scores, key_rows, preferred_element_type=F32) * scale
            grad_key = (
                lax.dot_general(grad_scores, query_rows, (((0,), (0,)), ((), ())), preferred_element_type=F32)
                * scale
            )
            grad_query = grad_query.astype(BF16)
            for index in range(grad_query.shape[0] // size):
                rows = slice((2 * index + odd) * size, (2 * index + odd + 1) * size)
                to_query[rows, columns] = grad_query[index * size : (index + 1) * size]
            if odd == 1:
                early = keys[0].shape[0]
                results = [(grad_key[early:], grad_value[early:], 1)]
                key_total, value_total = grad_key[:early], grad_value[:early]
            else:
                results = [(grad_key + key_total, grad_value + value_total, 0)]
            for grad_key, grad_value, part in results:
                blocks = grad_key.shape[0] // size // 2
                for index in range(blocks):
                    rows = slice((2 * index + part) * size, (2 * index + part + 1) * size)
                    near = slice(index * size, (index + 1) * size)
                    far = slice((blocks + index) * size, (blocks + index + 1) * size)
                    to_mine[rows, columns] = grad_key[near]
                    to_mine[rows, value_columns] = grad_value[near]
                    to_beside[rows, columns] = grad_key[far].astype(BF16)
                    to_beside[rows, value_columns] = grad_value[far].astype(BF16)


def attention_cost(query, products):
    elements = query.shape[0] * query.shape[0] * 3 // 2 * (query.shape[1] // HD)
    return pl.CostEstimate(
        flops=elements * HD * 2 * products, bytes_accessed=query.size * 16, transcendentals=elements
    )


def bias_shapes(query, keys):
    return [pltpu.VMEM((query.shape[0] // 2, keys * (odd + 1) // 2), F32) for odd in range(2)]


def attention_specs(count):
    return [pl.BlockSpec(memory_space=pltpu.SMEM)] + [pl.BlockSpec(memory_space=pltpu.VMEM)] * count


def attend(query, mine, beside, info):
    slopes, at_rows, at_keys, size = info
    return pl.pallas_call(
        functools.partial(attend_kernel, size),
        out_shape=[
            jax.ShapeDtypeStruct(query.shape, BF16),
            jax.ShapeDtypeStruct((query.shape[0], query.shape[1] // HD), F32),
        ],
        in_specs=attention_specs(5),
        out_specs=[pl.BlockSpec(memory_space=pltpu.VMEM)] * 2,
        scratch_shapes=bias_shapes(query, at_keys.shape[1]),
        compiler_params=pltpu.CompilerParams(vmem_limit_bytes=48 << 20),
        cost_estimate=attention_cost(query, 2),
    )(slopes, at_rows, at_keys, query, mine, beside)


def attend_back(query, mine, beside, log_totals, grad_mixed, info):
    slopes, at_rows, at_keys, size = info
    return pl.pallas_call(
        functools.partial(attend_back_kernel, size),
        out_shape=[
            jax.ShapeDtypeStruct(query.shape, BF16),
            jax.ShapeDtypeStruct(mine.shape, F32),
            jax.ShapeDtypeStruct(mine.shape, BF16),
        ],
        in_specs=attention_specs(7),
        out_specs=[pl.BlockSpec(memory_space=pltpu.VMEM)] * 3,
        scratch_shapes=bias_shapes(query, at_keys.shape[1]),
        compiler_params=pltpu.CompilerParams(vmem_limit_bytes=48 << 20),
        cost_estimate=attention_cost(query, 5),
    )(slopes, at_rows, at_keys, query, mine, beside, log_totals, grad_mixed)


def attention_info(lengths, slopes, size):
    block, core = lax.axis_index("b"), lax.axis_index("c")
    ends = jnp.cumsum(jnp.where(core == block, lengths, swap(lengths, "c")))
    across = lax.axis_size("r")
    steps = jnp.arange(size, dtype=jnp.int32)

    def spots(which, odd):
        return jnp.concatenate([((odd * across + place) * 2 + which) * size + steps for place in axis_order("r")])

    columns, keys = [], []
    for odd in range(2):
        place = spots(core, odd)
        start = jnp.max(jnp.where(place[:, None] >= ends[None, :], ends[None, :], 0), axis=1)
        columns += [place, start]
        keys += [spots(which, odd) for which in axis_order("c")]
    at_rows = jnp.stack(columns, 1).astype(F32)
    at_keys = jnp.concatenate(keys)[None, :].astype(F32)
    return slopes, at_rows, at_keys, size


def local(
    activations,
    lengths,
    cotangent,
    gain_attn,
    shift_attn,
    w_query,
    b_query,
    w_key,
    w_value,
    b_value,
    w_out,
    b_out,
    gain_ffn,
    shift_ffn,
    w_up,
    b_up,
    w_down,
    b_down,
):
    block, place = lax.axis_index("b"), lax.axis_index("r")
    across = lax.axis_size("r")
    shards = [block * across + place, (1 - block) * across + place]
    head_width = w_query.shape[2]
    head_count = head_width // HD
    hidden_width = w_up.shape[2]

    head_ids = jnp.concatenate(
        [shard * head_count + jnp.arange(head_count, dtype=jnp.int32) for shard in shards]
    ).astype(F32)
    slopes = 2.0 ** (-8.0 * (head_ids + 1.0) / H)
    info = attention_info(lengths[0], slopes, activations.shape[0] // 2)

    bias_own = jnp.concatenate([b_query, b_value], 1)
    bias_other = swap(bias_own, "b")

    used, results = {}, {}
    work = Background()
    for layer in range(LAYERS):
        work.add(
            fetch_attn(work, used, layer, w_query, w_key, w_value, w_out),
            FETCH_ATTN[layer],
        )
        work.add(fetch_ffn(work, used, layer, w_up, w_down), FETCH_FFN[layer])

    def move(name, steps, value):
        token, span = yield
        steps = steps(value, token)
        work.expect(next(steps), span)
        results[name] = next(steps)

    moving = to_chunks(activations, None, lambda value: work.at("r", value))
    next(moving)
    stream = work.at("s", next(moving).astype(F32))
    work.add(move("cotangent", to_chunks, cotangent), (COTANGENT,))

    def rows_of(array, first, last):
        size = array.shape[0] // across
        return array[first * size : last * size]

    stored = []
    zero = jnp.zeros((2 * head_width,), F32)
    for layer in range(LAYERS):
        bias_query = jnp.concatenate([bias_own[layer, :head_width], bias_other[layer, :head_width]])
        bias_kv = jnp.concatenate([zero, bias_own[layer, head_width:], bias_other[layer, head_width:]])
        bias_up = [
            lax.dynamic_slice_in_dim(b_up[layer], shard * hidden_width, hidden_width, 0) for shard in shards
        ]
        unit, inverse = norm_parts(stream)
        inputs = gather_rows((unit * gain_attn[layer] + shift_attn[layer]).astype(BF16), work, str(layer) + "a")
        weight_query, weight_kv, weight_out = used["attn", layer]
        mine = (dot(inputs, weight_kv) + bias_kv).astype(BF16)
        mine = work.at(str(layer) + "b", mine)
        beside = swap(mine, "c")
        query = (dot(inputs, weight_query) + bias_query).astype(BF16)
        mixed, log_totals = attend(query, mine, beside, info)
        middle = stream + (
            scatter_rows(lambda first, last: dot(rows_of(mixed, first, last), weight_out), work, str(layer) + "c") + b_out[layer]
        )
        unit_mid, inverse_mid = norm_parts(middle)
        inputs_mid = gather_rows((unit_mid * gain_ffn[layer] + shift_ffn[layer]).astype(BF16), work, str(layer) + "d")
        ups, downs = zip((w_up[layer], w_down[layer]), used["ffn", layer])
        hidden = [dot(inputs_mid, up) + bias for up, bias in zip(ups, bias_up)]
        active = [gelu_tanh(value).astype(BF16) for value in hidden]
        hidden = [value.astype(BF16) for value in hidden]
        stream = middle + (
            scatter_rows(lambda first, last: sum(dot(rows_of(value, first, last), down) for value, down in zip(active, downs)),
                work, str(layer) + "e") + b_down[layer]
        )
        stored.append(
            (
                unit,
                inverse,
                inputs,
                query,
                mine,
                beside,
                mixed,
                log_totals,
                unit_mid,
                inverse_mid,
                inputs_mid,
                hidden,
                active,
            )
        )
    work.add(move("activations_out", from_chunks, stream.astype(BF16)), (ACTIVATIONS_OUT,))
    grad_stream = results["cotangent"].astype(F32)
    small = {}
    for layer in reversed(range(LAYERS)):
        weight_query, weight_kv, weight_out = used["attn", layer]
        ups, downs = zip((w_up[layer], w_down[layer]), used["ffn", layer])
        (
            unit,
            inverse,
            inputs,
            query,
            mine,
            beside,
            mixed,
            log_totals,
            unit_mid,
            inverse_mid,
            inputs_mid,
            hidden,
            active,
        ) = stored[layer]
        grad_branch = grad_stream.astype(BF16)
        grad_b_down = jnp.sum(grad_branch, axis=0, dtype=F32)
        branch_all = gather_rows(grad_branch, work, str(layer) + "f")
        grad_hidden = [
            jax.vjp(gelu_tanh, value.astype(F32))[1](dot_nt(branch_all, down))[0].astype(BF16)
            for value, down in zip(hidden, downs)
        ]
        work.add(
            reduce_weights(
                work,
                results,
                "ffn",
                layer,
                ([(inputs_mid, jnp.concatenate(grad_hidden, 1))], [(branch_all, jnp.concatenate(active, 1))]),
                ((0, 0, hidden_width, False), (1, 0, hidden_width, True)),
            ),
            REDUCE_FFN[layer],
        )
        grad_normed_mid = scatter_rows(
            lambda first, last: sum(dot_nt(rows_of(value, first, last), up) for value, up in zip(grad_hidden, ups)),
            work,
            str(layer) + "g",
        )
        grad_b_up = jnp.concatenate([jnp.sum(value, axis=0, dtype=F32) for value in grad_hidden])
        grad_gain_ffn = jnp.sum(grad_normed_mid * unit_mid, axis=0)
        grad_shift_ffn = jnp.sum(grad_normed_mid, axis=0)
        grad_middle = grad_stream + norm_back(grad_normed_mid, unit_mid, inverse_mid, gain_ffn[layer])
        grad_attn = grad_middle.astype(BF16)
        grad_b_out = jnp.sum(grad_attn, axis=0, dtype=F32)
        attn_all = gather_rows(grad_attn, work, str(layer) + "h")
        grad_mixed = dot_nt(attn_all, weight_out).astype(BF16)
        grad_query, grad_mine, grad_beside = attend_back(query, mine, beside, log_totals, grad_mixed, info)
        grad_beside = work.at(str(layer) + "i", grad_beside)
        grad_kv = (grad_mine + swap(grad_beside, "c").astype(F32)).astype(BF16)
        work.add(
            reduce_weights(
                work,
                results,
                "attn",
                layer,
                (
                    [(inputs, grad_kv[:, : 2 * head_width]), (inputs, grad_kv[:, 2 * head_width :])],
                    [(inputs, grad_query), (attn_all, mixed)],
                ),
                (
                    (1, 0, head_width, False),
                    (0, 0, head_width, False),
                    (0, head_width, head_width, False),
                    (1, head_width, head_width, True),
                ),
            ),
            REDUCE_ATTN[layer],
        )
        grad_normed = scatter_rows(
            lambda first, last: dot_nt(rows_of(grad_query, first, last), weight_query)
            + dot_nt(rows_of(grad_kv, first, last), weight_kv),
            work,
            str(layer) + "j",
        )
        grad_b_query = jnp.sum(grad_query, axis=0, dtype=F32)
        grad_b_value = jnp.sum(grad_kv[:, 2 * head_width :], axis=0, dtype=F32)
        grads_in = grad_normed
        grad_gain_attn = jnp.sum(grad_normed * unit, axis=0)
        grad_shift_attn = jnp.sum(grad_normed, axis=0)
        grad_stream = grad_middle + norm_back(grad_normed, unit, inverse, gain_attn[layer])

        def spread(values, total):
            width = values.shape[0] // 2
            result = jnp.zeros((total,), F32)
            for index, shard in enumerate(shards):
                result = lax.dynamic_update_slice_in_dim(
                    result, values[index * width : (index + 1) * width], shard * width, 0
                )
            return result

        whole = head_width * 2 * across
        packed = jnp.concatenate(
            [
                grad_gain_attn,
                grad_shift_attn,
                grad_b_out,
                grad_gain_ffn,
                grad_shift_ffn,
                grad_b_down,
                spread(grad_b_query, whole),
                spread(grad_b_value, whole),
                spread(grad_b_up, b_up.shape[1]),
            ]
        )
        small[layer] = packed.reshape(-1, 128)

    work.add(sum_small(work, results, jnp.stack([small[layer] for layer in range(LAYERS)])), SUM_SMALL)
    work.add(move("input_grad", from_chunks, grad_stream.astype(BF16)), ("t3",))
    work.at("t1", grads_in)
    for step in range(2, 7):
        work.at("t" + str(step), work.latest)
    assert not work.tasks
    attn_outs, ffn_outs = results["attn"], results["ffn"]
    table = results["small"].reshape(LAYERS, -1)
    wide = gain_attn.shape[1]
    shared = [table[:, index * wide : (index + 1) * wide] for index in range(6)]
    begin = 6 * wide
    whole = head_width * 2 * across
    home = shards[0]
    all_b_query = lax.dynamic_slice_in_dim(table[:, begin : begin + whole], home * head_width, head_width, 1)
    begin += whole
    all_b_value = lax.dynamic_slice_in_dim(table[:, begin : begin + whole], home * head_width, head_width, 1)
    begin += whole
    all_b_up = lax.dynamic_slice_in_dim(table[:, begin:], home * hidden_width, hidden_width, 1)
    return (
        results["activations_out"],
        results["input_grad"],
        shared[0],
        shared[1],
        attn_outs[0],
        all_b_query,
        attn_outs[1],
        attn_outs[2],
        all_b_value,
        attn_outs[3],
        shared[2],
        shared[3],
        shared[4],
        ffn_outs[0],
        all_b_up,
        ffn_outs[1],
        shared[5],
    )


def solution(mesh):
    groups, parts = mesh.shape["dp"], mesh.shape["mp"]
    fine = Mesh(
        mesh.devices.reshape(2, groups // 4, 2, 2, parts // 2), ("ky", "kx", "c", "b", "r")
    )
    dp, mp = ("ky", "kx", "c"), ("b", "r")
    rows, whole = P(dp + mp, None), P()
    columns3, columns2, rows3 = P(None, None, mp), P(None, mp), P(None, mp, None)
    return jax.shard_map(
        local,
        mesh=fine,
        in_specs=(
            rows,
            P(dp, None),
            rows,
            whole,
            whole,
            columns3,
            columns2,
            columns3,
            columns3,
            columns2,
            rows3,
            whole,
            whole,
            whole,
            columns3,
            whole,
            rows3,
            whole,
        ),
        out_specs=(
            rows,
            rows,
            whole,
            whole,
            columns3,
            columns2,
            columns3,
            columns3,
            columns2,
            rows3,
            whole,
            whole,
            whole,
            columns3,
            columns2,
            rows3,
            whole,
        ),
        check_vma=False,
    )
```
